768 devices in a mesh: tensor: 24 (over z, core), dp: 32 (over x, y).
Axes of the slice: x: 4, y: 8, z: 12, core: 2. Of those that a mesh axis runs over, the one named last changes fastest.
Arguments:
- gate_pre: bfloat16 [4096, 15360], P('dp', 'tensor'), may hold values from -8 to 8
- up_pre: bfloat16 [4096, 15360], P('dp', 'tensor'), may hold values from -6 to 6
- out_grad: bfloat16 [4096, 6144], P('dp', 'tensor'), may hold values from -6 to 6
- weight_slots: bfloat16 [1728, 128, 128], P('tensor'), may hold values from -0.15625 to 0.15625
- holder_blocks: int32 [1728, 2], P('tensor'), may hold values from 0 to 119, as said below
- holder_live_slots: int32 [576], P('tensor'), may hold values from 2 to 3, as said below
- row_columns: int32 [120, 12], P('tensor'), may hold values from 0 to 47, as said below
Outputs:
- gate_grad: bfloat16 [4096, 15360], P('dp', 'tensor')
- up_grad: bfloat16 [4096, 15360], P('dp', 'tensor')
- weight_grad: bfloat16 [1440, 16384], P('tensor', 'dp')
The draws below stay inside these ranges and needn't reach their ends.
Inputs may be any that keep to these rules, and one draw needn't show every extreme that they name: `holder_blocks`: slot s of holder h (row h * 72 + s) names a live block (its row block, then its column block, a column that row_columns lists for that row) when it is live by holder_live_slots, and (0, 0) otherwise; a live slot's row block lies among those of tensor index s // 3, that is from (s // 3) * 5 on; every live block is named by exactly one slot. `holder_live_slots`: entry h * 24 + o counts the live slots of holder h for the row blocks of tensor index o; for each o they sum over h to 60; some holder has 3 in every entry. `row_columns`: each row holds 12 distinct column blocks in rising order.
All inputs are finite; a program needn't handle non-finite values.
Results may differ from the reference program's by a relative error of at most 0.022.
Values may be sent and summed in bfloat16 or wider, within the bound.
A program may use at most 64 MiB of HBM per device.

```python
import jax
import jax.numpy as jnp
from jax import lax

D = 6144
FF = 15360
BLOCK = 128
DCOL = 48
RB = 120
KEEP = 12
BLOCKS_LIVE = 1440
CAP = 3
SLOTS = 72
TOKENS = 4096
N_TENSOR = 24


def layout(key):
    average = BLOCKS_LIVE // N_TENSOR
    pair_total = 2 * average // N_TENSOR
    lowest = pair_total - CAP
    row_keys = jax.random.split(jax.random.fold_in(key, 101), RB)
    shuffled = jax.vmap(lambda one_key: jax.random.permutation(one_key, DCOL))(row_keys)
    columns = jnp.sort(shuffled[:, :KEEP], axis=1).astype(jnp.int32)
    pairing = jax.random.permutation(jax.random.fold_in(key, 102), N_TENSOR)
    first = jax.random.randint(jax.random.fold_in(key, 103), (N_TENSOR // 2, N_TENSOR), lowest, CAP + 1)
    first = first.at[0].set(CAP)
    counts = jnp.zeros((N_TENSOR, N_TENSOR), jnp.int32)
    counts = counts.at[pairing[0::2]].set(first).at[pairing[1::2]].set(pair_total - first)
    offsets = jnp.cumsum(counts, axis=0) - counts
    owner_keys = jax.random.split(jax.random.fold_in(key, 104), N_TENSOR)
    orders = jax.vmap(lambda one_key: jax.random.permutation(one_key, average))(owner_keys).astype(jnp.int32)
    slot_ids = jnp.arange(SLOTS, dtype=jnp.int32)
    owner = slot_ids // CAP
    place = slot_ids % CAP
    validity = place[None, :] < counts[:, owner]
    local_index = jnp.clip(offsets[:, owner] + place[None, :], 0, average - 1)
    owner_grid = jnp.broadcast_to(owner[None, :], (N_TENSOR, SLOTS))
    block_ids = owner_grid * average + orders[owner_grid, local_index]
    row_block = block_ids // KEEP
    col_block = columns[row_block, block_ids % KEEP]
    row_block = jnp.where(validity, row_block, 0)
    col_block = jnp.where(validity, col_block, 0)
    blocks = jnp.stack([row_block, col_block], axis=-1).reshape(N_TENSOR * SLOTS, 2).astype(jnp.int32)
    return (columns, blocks, counts.reshape(N_TENSOR * N_TENSOR).astype(jnp.int32))


def draw_holder_blocks(key, part):
    columns, blocks, counts = layout(key)
    return blocks


def draw_holder_live_slots(key, part):
    columns, blocks, counts = layout(key)
    return counts


def draw_row_columns(key, part):
    columns, blocks, counts = layout(key)
    return columns


def levels(own_key, shape, shards, least, largest):
    def one(dim, blocks):
        heights = jax.random.uniform(jax.random.fold_in(jax.random.fold_in(own_key, 6), dim), (blocks,), jnp.float32, least / len(shards), largest / len(shards))
        return jnp.repeat(jnp.exp(heights), shape[dim] // blocks).reshape((-1,) + (1,) * (len(shape) - dim - 1))

    gain = one(*shards[0])
    for cut in shards[1:]:
        gain = gain * one(*cut)
    return gain


def bell_draw(stream_key, extent, width, reach, shards=(), kind=jnp.bfloat16):
    result = width * jax.random.normal(stream_key, extent, jnp.float32)
    if shards:
        result = result * levels(stream_key, extent, shards, -0.22, 0.18)
    return jnp.clip(result, -reach, reach).astype(kind)


def setup_inputs(seed: int = 0) -> dict:
    keys = jax.random.split(jax.random.key(seed), 8)
    gate_pre = bell_draw(keys[0], (TOKENS, FF), 1.5, 8.0, ((0, 32), (1, 24)))
    up_pre = bell_draw(keys[1], (TOKENS, FF), 1.0, 6.0, ((0, 32), (1, 24)))
    out_grad = bell_draw(keys[2], (TOKENS, D), 1.0, 6.0, ((0, 32), (1, 24)))
    weight_slots = bell_draw(keys[3], (N_TENSOR * SLOTS, BLOCK, BLOCK), (KEEP * BLOCK) ** -0.5, 0.15625, ((0, 24),))
    holder_blocks = draw_holder_blocks(jax.random.fold_in(keys[7], 71), 0)
    holder_live_slots = draw_holder_live_slots(jax.random.fold_in(keys[7], 71), 0)
    row_columns = draw_row_columns(jax.random.fold_in(keys[7], 71), 0)
    return dict(gate_pre=gate_pre, up_pre=up_pre, out_grad=out_grad, weight_slots=weight_slots, holder_blocks=holder_blocks, holder_live_slots=holder_live_slots, row_columns=row_columns)


def gating(gate_pre, up_pre):
    gate_value = gate_pre.astype(jnp.float32)
    sigmoid_gate = jax.nn.sigmoid(gate_value)
    activation = gate_value * sigmoid_gate
    slope_value = sigmoid_gate * (1.0 + gate_value * (1.0 - sigmoid_gate))
    return (activation, slope_value, up_pre.astype(jnp.float32))

def reference(gate_pre, up_pre, out_grad, weight_slots, holder_blocks, holder_live_slots, row_columns):
    activation, slope_value, up_value = gating(gate_pre, up_pre)
    hidden = (activation * up_value).astype(jnp.bfloat16)
    column_count = out_grad.shape[1] // BLOCK
    rows_all = FF // BLOCK
    grad_blocks = out_grad.astype(jnp.float32).reshape(TOKENS, column_count, BLOCK)
    slot_ids = jnp.arange(SLOTS, dtype=jnp.int32)

    def holder_term(running, holder):
        start_slot = (holder * SLOTS).astype(jnp.int32)
        weights = lax.dynamic_slice_in_dim(weight_slots, start_slot, SLOTS, 0).astype(jnp.float32)
        coords = lax.dynamic_slice_in_dim(holder_blocks, start_slot, SLOTS, 0)
        counts = lax.dynamic_slice_in_dim(holder_live_slots, (holder * N_TENSOR).astype(jnp.int32), N_TENSOR, 0)
        alive_flags = slot_ids % CAP < counts[slot_ids // CAP]
        picked = grad_blocks[:, coords[:, 1], :]
        contrib = jnp.einsum('tsk,sjk->tsj', picked, weights)
        contrib = contrib * alive_flags.astype(jnp.float32)[None, :, None]
        partial_value = jnp.zeros((TOKENS, rows_all, BLOCK), jnp.float32).at[:, coords[:, 0], :].add(contrib)
        rounded = lax.optimization_barrier(partial_value.astype(jnp.bfloat16))
        return (running + rounded.astype(jnp.float32), None)
    running, _ = lax.scan(holder_term, jnp.zeros((TOKENS, rows_all, BLOCK), jnp.float32), jnp.arange(N_TENSOR, dtype=jnp.int32))
    hidden_grad = running.reshape(TOKENS, FF)
    gate_grad = (hidden_grad * up_value * slope_value).astype(jnp.bfloat16)
    up_grad = (hidden_grad * activation).astype(jnp.bfloat16)
    hidden_blocks = hidden.astype(jnp.float32).reshape(TOKENS, rows_all, BLOCK)

    def row_grad(row_block):
        left_rows = hidden_blocks[:, row_block, :]
        right_rows = grad_blocks[:, row_columns[row_block], :]
        return jnp.einsum('ta,tkb->kab', left_rows, right_rows).reshape(KEEP, BLOCK * BLOCK)
    block_terms = lax.map(row_grad, jnp.arange(rows_all, dtype=jnp.int32))
    weight_grad = block_terms.reshape(rows_all * KEEP, BLOCK * BLOCK).astype(jnp.bfloat16)
    return (gate_grad, up_grad, weight_grad)
```

```python
import jax
import jax.numpy as jnp
from jax import lax
from jax.experimental import pallas as pl
from jax.experimental.pallas import tpu as pltpu
from jax.sharding import PartitionSpec as P

MESH = pl.DeviceIdType.MESH
NX, NY, NZ = 4, 8, 12
NT = 2 * NZ
RZ, RY = NZ // 2, NY // 2
ROWS, KEEP, B = 5, 12, 128
HALF = KEEP // 2 * B
BF, F32 = jnp.bfloat16, jnp.float32
CUT = 128
NROW = ROWS * KEEP * 4


def kernel(
    gate, up, og, w_hbm, hb, live, rc,
    gg, ug, wg,
    og_all, slab, msg, recv, comm_x, w_all, act, slope_up, hid_t, part, buf_x, fin_x, snd_x, yin, snd_y, rcv_y,
    slab_sem, z_send, z_recv, s_send, s_recv, a_send, a_recv, gx_send, gx_recv, gy_send, gy_recv,
    rx_send, rx_recv, ry_send, ry_recv,
):
    t, d = lax.axis_index("tensor"), lax.axis_index("dp")
    z, c = lax.div(t, 2), lax.rem(t, 2)
    x, y = lax.div(d, NY), lax.rem(d, NY)

    def zdev(k):
        return {"tensor": lax.rem(z + k + NZ, NZ) * 2 + c}

    def xdev(k):
        return {"dp": lax.rem(x + k + NX, NX) * NY + y}

    def ydev(k):
        return {"dp": x * NY + lax.rem(y + k + NY, NY)}

    sibling = {"tensor": z * 2 + (1 - c)}

    def copy(src, dst, ss, rs, dev):
        return pltpu.make_async_remote_copy(
            src_ref=src, dst_ref=dst, send_sem=ss, recv_sem=rs, device_id=dev, device_id_type=MESH
        )

    slab_copy = pltpu.make_async_copy(w_hbm.at[:, pl.ds(pl.multiple_of(y * 16, 16), 16), :], slab, slab_sem)
    slab_copy.start()

    barrier = pltpu.get_barrier_semaphore()

    def greet(s, carry):
        pl.semaphore_signal(barrier, inc=1, device_id={"tensor": lax.rem(t + s, NT)}, device_id_type=MESH)
        return carry

    lax.fori_loop(1, NT, greet, 0)
    for k in (1, 2, 3):
        pl.semaphore_signal(barrier, inc=1, device_id=xdev(k), device_id_type=MESH)
    for k in (1, -1):
        pl.semaphore_signal(barrier, inc=1, device_id=ydev(k), device_id_type=MESH)
    pend = []

    og_all[2 * t] = og[:, :B]
    og_all[2 * t + 1] = og[:, B:]
    pl.semaphore_wait(barrier, NT - 1 + 3 + 2)

    def zslot(k, cc, h):
        return 2 * (lax.rem(z + k + NZ, NZ) * 2 + cc) + h

    def chunks(s):
        if s < RZ:
            return [(0, 0), (1, 0), (0, 1), (1, 1)]
        return [(0, 0), (1, 1)]

    def z_start(s, e, h):
        sg = 1 if e == 0 else -1
        slot = og_all.at[zslot(-sg * (s - 1), c, h)]
        cp = copy(slot, slot, z_send.at[e, s - 1, h], z_recv.at[e, s - 1, h], zdev(sg))
        cp.start()
        pend.append(cp)

    def sib_start(s, e, h):
        sg = 1 if e == 0 else -1
        slot = og_all.at[zslot(-sg * s, c, h)]
        cp = copy(slot, slot, s_send.at[e, s, h], s_recv.at[e, s, h], sibling)
        cp.start()
        pend.append(cp)

    def sib_wait(s, e, h):
        sg = 1 if e == 0 else -1
        slot = og_all.at[zslot(-sg * s, 1 - c, h)]
        copy(slot, slot, s_send.at[e, s, h], s_recv.at[e, s, h], sibling).wait_recv()

    def z_step(s):
        for e, h in chunks(s):
            sg = 1 if e == 0 else -1
            slot = og_all.at[zslot(-sg * s, c, h)]
            copy(slot, slot, z_send.at[e, s - 1, h], z_recv.at[e, s - 1, h], zdev(sg)).wait_recv()
            if s < RZ and (e, h) in chunks(s + 1):
                z_start(s + 1, e, h)
            sib_start(s, e, h)

    for e, h in chunks(1):
        z_start(1, e, h)
    for h in (0, 1):
        sib_start(0, 0, h)

    slab_copy.wait()
    r_out = lax.broadcasted_iota(jnp.int32, (64, 192), 0)
    r_in = lax.broadcasted_iota(jnp.int32, (64, 192), 1)
    q = lax.rem(r_out, 16)
    pick = (
        (lax.div(r_out, 16) == lax.div(r_in, 48))
        & (lax.div(q, 4) == lax.div(lax.rem(r_in, 48), 16))
        & (q < 12)
        & (x * 4 + lax.rem(q, 4) == lax.rem(r_in, 16))
    )
    pick = jnp.where(pick, 1.0, 0.0).astype(BF)
    row16 = lax.broadcasted_iota(jnp.int32, (16, B), 0)

    def make_msg(m, carry):
        rows = slab[pl.ds(m * 12, 12)].reshape(192, B)
        picked = jnp.dot(pick, rows, preferred_element_type=F32)
        for u in range(4):
            o = m * 4 + u
            tile = picked[16 * u : 16 * u + 16]
            for s in range(3):
                key = (hb[o * 3 + s, 0] - o * ROWS) * 48 + hb[o * 3 + s, 1]
                key = jnp.where(s < live[o], key, -1).astype(F32)
                tile = jnp.where(row16 == 12 + s, key, tile)
            msg[o] = tile.astype(BF)
        return carry

    lax.fori_loop(0, NT // 4, make_msg, 0)
    recv[t] = msg[t]

    def a_copy(s):
        o = lax.rem(t + s, NT)
        return copy(msg.at[o], recv.at[t], a_send.at[s], a_recv.at[t], {"tensor": o})

    def a_start(s, carry):
        a_copy(s).start()
        return carry

    lax.fori_loop(1, NT, a_start, 0)

    for i in range(ROWS):
        g = gate[:, i * B : (i + 1) * B].astype(F32)
        u = up[:, i * B : (i + 1) * B].astype(F32)
        sig = 1.0 / (1.0 + jnp.exp(-g))
        a = g * sig
        act[:, i * B : (i + 1) * B] = a
        slope_up[:, i * B : (i + 1) * B] = u * (sig * (1.0 + g * (1.0 - sig)))
        hid_t[i] = (a * u).T.astype(BF)

    lane = lax.broadcasted_iota(jnp.int32, (8, 2 * B), 1)
    block_of = lax.div(lane, 4)
    keycol = jnp.full((8, 2 * B), -100.0, F32)
    for n in range(ROWS * KEEP):
        v = ((n // KEEP) * 48 + rc[n // KEEP, n % KEEP]) * 4
        keycol = jnp.where(block_of == n, v.astype(F32), keycol)
    keycol = (keycol + lax.rem(lane, 4).astype(F32))[0:1]

    z_step(1)
    z_step(2)

    def a_wait(s, carry):
        h = lax.rem(t + s, NT)
        copy(msg.at[h], recv.at[h], a_send.at[s], a_recv.at[h], {"tensor": h}).wait_recv()
        return carry

    lax.fori_loop(1, NT, a_wait, 0)

    got = recv[...]
    gotf = got.astype(F32)
    rr = lax.broadcasted_iota(jnp.int32, (NT, 16, B), 1)
    keyrow = jnp.where(
        rr < 4, gotf[:, 12:13, :], jnp.where(rr < 8, gotf[:, 13:14, :], jnp.where(rr < 12, gotf[:, 14:15, :], -1000.0))
    )
    keyrow = (keyrow * 4.0 + lax.rem(rr, 4).astype(F32)).reshape(NT * 16, B)
    got = got.reshape(NT * 16, B)
    for v in range(2):
        hot = jnp.where(keyrow == keycol[:, v * B : (v + 1) * B], 1.0, 0.0).astype(BF)
        res = lax.dot_general(hot, got, (((0,), (0,)), ((), ())), preferred_element_type=F32).astype(BF)
        n_tiles = 8 if v == 0 else 7
        comm_x[x, 8 * v : 8 * v + n_tiles] = res[: 16 * n_tiles].reshape(n_tiles, 16, B)

    for k in (1, 3, 2):
        cp = copy(comm_x.at[x], comm_x.at[x], gx_send.at[k - 1], gx_recv.at[k - 1], xdev(k))
        cp.start()
        pend.append(cp)

    z_step(3)
    z_step(4)

    for k in (1, 3, 2):
        src = comm_x.at[lax.rem(x - k + NX, NX)]
        copy(src, src, gx_send.at[k - 1], gx_recv.at[k - 1], xdev(k)).wait_recv()
    p_out = lax.broadcasted_iota(jnp.int32, (64, 64), 0)
    p_in = lax.broadcasted_iota(jnp.int32, (64, 64), 1)
    swap = (
        (lax.div(p_out, 16) == lax.rem(lax.div(p_in, 4), 4))
        & (lax.rem(lax.div(p_out, 4), 4) == lax.div(p_in, 16))
        & (lax.rem(p_out, 4) == lax.rem(p_in, 4))
    )
    swap = jnp.where(swap, 1.0, 0.0).astype(BF)
    for g in range(15):
        res = jnp.dot(swap, comm_x[:, g].reshape(64, B), preferred_element_type=F32).astype(BF)
        for u in range(4):
            n = 4 * g + u
            i, k = n // KEEP, n % KEEP
            w_all[y, k // 6, i, :, (k % 6) * B : (k % 6 + 1) * B] = res[16 * u : 16 * u + 16]

    def y_chunks(s):
        if s < RY:
            return [(0, 0), (1, 1), (0, 1), (1, 0)]
        return [(0, 0), (1, 1)]

    def gy_slot(k, h):
        return w_all.at[lax.rem(y + k + NY, NY), h]

    def gy_start(s, e, h):
        sg = 1 if e == 0 else -1
        slot = gy_slot(-sg * (s - 1), h)
        cp = copy(slot, slot, gy_send.at[e, s - 1, h], gy_recv.at[e, s - 1, h], ydev(sg))
        cp.start()
        pend.append(cp)

    def gy_step(s):
        for e, h in y_chunks(s):
            sg = 1 if e == 0 else -1
            slot = gy_slot(-sg * s, h)
            copy(slot, slot, gy_send.at[e, s - 1, h], gy_recv.at[e, s - 1, h], ydev(sg)).wait_recv()
            if s < RY and (e, h) in y_chunks(s + 1):
                gy_start(s + 1, e, h)

    for e, h in y_chunks(1):
        gy_start(1, e, h)

    z_step(5)
    z_step(6)
    for h in (0, 1):
        sib_wait(0, 0, h)
    for s in range(1, RZ + 1):
        for e, h in chunks(s):
            sib_wait(s, e, h)

    def products(h):
        def one(i, carry):
            for p in range(3):
                k = h * 6 + 2 * p
                pair = jnp.concatenate([og_all[rc[i, k]], og_all[rc[i, k + 1]]], axis=1)
                res = jnp.dot(hid_t[i], pair, preferred_element_type=F32).astype(BF)
                part[:, h, i, :, p * 256 : (p + 1) * 256] = res.reshape(NX, 32, 256)
            return carry

        lax.fori_loop(0, ROWS, one, 0)

    def xi(k):
        return lax.rem(x + k + NX, NX)

    def rx(e, j, src, dst):
        return copy(src, dst, rx_send.at[e, j], rx_recv.at[e, j], xdev(1 if e == 0 else -1))

    def rx_start(*args):
        cp = rx(*args)
        cp.start()
        pend.append(cp)

    products(0)
    rx_start(0, 0, part.at[xi(2), 0], buf_x.at[0])
    rx_start(1, 1, part.at[xi(-1), 0], fin_x.at[1, 0])
    products(1)
    rx_start(1, 0, part.at[xi(2), 1], buf_x.at[1])
    rx_start(0, 1, part.at[xi(1), 1], fin_x.at[0, 1])
    gy_step(1)
    for e in (0, 1):
        rx(e, 0, part.at[xi(2), e], buf_x.at[e]).wait_recv()
        mine = part[xi(1 if e == 0 else -1), e].astype(F32)
        snd_x[e] = (mine + buf_x[e].astype(F32)).astype(BF)
        rx_start(e, 2, snd_x.at[e], fin_x.at[e, e])
    gy_step(2)
    gy_step(3)
    gy_step(4)

    def hidden_grad(i, carry):
        total = jnp.zeros((B, B), F32)
        for h in range(2):
            left = jnp.concatenate([og_all[rc[i, h * 6 + k]] for k in range(6)], axis=1)
            right = w_all[:, h, i].reshape(B, HALF)
            total = total + lax.dot_general(
                left, right, (((1,), (1,)), ((), ())), preferred_element_type=F32
            )
        cols = pl.ds(pl.multiple_of(i * B, B), B)
        gg[:, cols] = (total * slope_up[:, cols]).astype(BF)
        ug[:, cols] = (total * act[:, cols]).astype(BF)
        return carry

    lax.fori_loop(0, ROWS, hidden_grad, 0)

    for e in (0, 1):
        rx(e, 1, part.at[xi(1), 1 - e], fin_x.at[e, 1 - e]).wait_recv()
        rx(e, 2, snd_x.at[e], fin_x.at[e, e]).wait_recv()
    low = lax.broadcasted_iota(jnp.int32, (4, 8, B), 1) < 4
    for h in range(2):
        for i in range(ROWS):
            own = part[x, h, i].astype(F32) + fin_x[0, h, i].astype(F32) + fin_x[1, h, i].astype(F32)
            own = own.reshape(4, 8, HALF)
            for p in range(3):
                a0 = own[:, :, 2 * p * B : (2 * p + 1) * B]
                a1 = own[:, :, (2 * p + 1) * B : (2 * p + 2) * B]
                d0 = jnp.where(low, a0, pltpu.roll(a1, 4, 1))
                d1 = jnp.where(low, pltpu.roll(a0, 4, 1), a1)
                first = (i * KEEP + h * 6 + 2 * p) * 4
                yin[:, 0, first : first + 8, :] = d0
                yin[:, 1, first : first + 8, :] = d1

    span = [pl.ds(0, CUT), pl.ds(CUT, NROW - CUT)]

    def yblock(k, h):
        yy = lax.rem(y + k + NY, NY)
        return yin[lax.div(yy, 2), lax.rem(yy, 2), span[h], :]

    def ry(s, e, h):
        return copy(
            snd_y.at[e, s - 1, span[h], :], rcv_y.at[e, s - 1, span[h], :],
            ry_send.at[e, s - 1, h], ry_recv.at[e, s - 1, h], ydev(1 if e == 0 else -1),
        )

    for s in range(1, RY + 1):
        for e, h in ([(0, 0), (1, 1)] if s == 1 else [(0, 1), (1, 0), (0, 0), (1, 1)] if s == 2 else [(0, 0), (1, 1), (0, 1), (1, 0)]):
            sg = 1 if e == 0 else -1
            v = yblock(sg * (RY + 1 - s), h)
            if s > 2 or (s == 2 and e == h):
                ry(s - 1, e, h).wait_recv()
                v = v + rcv_y[e, s - 2, span[h], :].astype(F32)
            snd_y[e, s - 1, span[h], :] = v.astype(BF)
            cp = ry(s, e, h)
            cp.start()
            pend.append(cp)
    for h in (0, 1):
        for e in (0, 1):
            ry(RY, e, h).wait_recv()
        v = yblock(0, h) + rcv_y[0, RY - 1, span[h], :].astype(F32) + rcv_y[1, RY - 1, span[h], :].astype(F32)
        wg[span[h], :] = v.astype(BF)

    def a_done(s, carry):
        a_copy(s).wait_send()
        return carry

    lax.fori_loop(1, NT, a_done, 0)
    for cp in pend:
        cp.wait_send()


def local(gate_pre, up_pre, out_grad, weight_slots, holder_blocks, holder_live_slots, row_columns):
    vmem = pl.BlockSpec(memory_space=pltpu.VMEM)
    smem = pl.BlockSpec(memory_space=pltpu.SMEM)
    dma = pltpu.SemaphoreType.DMA
    gate_grad, up_grad, weight_grad = pl.pallas_call(
        kernel,
        out_shape=(
            jax.ShapeDtypeStruct(gate_pre.shape, BF),
            jax.ShapeDtypeStruct(gate_pre.shape, BF),
            jax.ShapeDtypeStruct((NROW, B), BF),
        ),
        in_specs=[vmem, vmem, vmem, pl.BlockSpec(memory_space=pl.ANY), smem, smem, smem],
        out_specs=(vmem, vmem, vmem),
        scratch_shapes=[
            pltpu.VMEM((2 * NT, B, B), BF),
            pltpu.VMEM((3 * NT, 16, B), BF),
            pltpu.VMEM((NT, 16, B), BF),
            pltpu.VMEM((NT, 16, B), BF),
            pltpu.VMEM((NX, 15, 16, B), BF),
            pltpu.VMEM((NY, 2, ROWS, 16, HALF), BF),
            pltpu.VMEM((B, ROWS * B), F32),
            pltpu.VMEM((B, ROWS * B), F32),
            pltpu.VMEM((ROWS, B, B), BF),
            pltpu.VMEM((NX, 2, ROWS, 32, HALF), BF),
            pltpu.VMEM((2, ROWS, 32, HALF), BF),
            pltpu.VMEM((2, 2, ROWS, 32, HALF), BF),
            pltpu.VMEM((2, ROWS, 32, HALF), BF),
            pltpu.VMEM((NY // 2, 2, NROW, B), F32),
            pltpu.VMEM((2, RY, NROW, B), BF),
            pltpu.VMEM((2, RY, NROW, B), BF),
            dma,
            dma((2, RZ, 2)), dma((2, RZ, 2)),
            dma((2, RZ + 1, 2)), dma((2, RZ + 1, 2)),
            dma((NT,)), dma((NT,)),
            dma((3,)), dma((3,)),
            dma((2, RY, 2)), dma((2, RY, 2)),
            dma((2, 3)), dma((2, 3)),
            dma((2, RY, 2)), dma((2, RY, 2)),
        ],
        compiler_params=pltpu.CompilerParams(
            collective_id=0, has_side_effects=True, vmem_limit_bytes=40 * 1024 * 1024
        ),
        cost_estimate=pl.CostEstimate(flops=600_000_000, bytes_accessed=4_000_000, transcendentals=82_000),
    )(gate_pre, up_pre, out_grad, weight_slots, holder_blocks, holder_live_slots, row_columns)
    return gate_grad, up_grad, weight_grad.reshape(ROWS * KEEP, 4 * B)


def solution(mesh):
    placed = (
        P("dp", "tensor"),
        P("dp", "tensor"),
        P("dp", "tensor"),
        P("tensor", None, None),
        P("tensor", None),
        P("tensor"),
        P("tensor", None),
    )
    return jax.shard_map(
        local,
        mesh=mesh,
        in_specs=placed,
        out_specs=(P("dp", "tensor"), P("dp", "tensor"), P("tensor", "dp")),
        check_vma=False,
    )
```

```python
import jax
import jax.numpy as jnp
from jax import lax
from jax.experimental import pallas as pl
from jax.experimental.pallas import tpu as pltpu
from jax.sharding import PartitionSpec as P

MESH = pl.DeviceIdType.MESH
NX, NY, NZ = 4, 8, 12
NT = 2 * NZ
RZ, RY = NZ // 2, NY // 2
ROWS, KEEP, B = 5, 12, 128
HALF = KEEP // 2 * B
BF, F32 = jnp.bfloat16, jnp.float32
CUT = 128
NROW = ROWS * KEEP * 4


def kernel(
    gate_hbm, up_hbm, og_hbm, w_hbm, hb_hbm, live_hbm, rc_hbm,
    gg_hbm, ug_hbm, wg_hbm,
    gate, up, og, hb, live, rc, gg, ug, wg,
    og_all, slab, msg, recv, comm_x, w_all, act, slope_up, hid_t, part, buf_x, fin_x, snd_x, yin, snd_y, rcv_y,
    in_sem, out_sem, z_send, z_recv, s_send, s_recv, a_send, a_recv, gx_send, gx_recv, gy_send, gy_recv,
    rx_send, rx_recv, ry_send, ry_recv,
):
    t, d = lax.axis_index("tensor"), lax.axis_index("dp")
    z, c = lax.div(t, 2), lax.rem(t, 2)
    x, y = lax.div(d, NY), lax.rem(d, NY)

    def zdev(k):
        return {"tensor": lax.rem(z + k + NZ, NZ) * 2 + c}

    def xdev(k):
        return {"dp": lax.rem(x + k + NX, NX) * NY + y}

    def ydev(k):
        return {"dp": x * NY + lax.rem(y + k + NY, NY)}

    sibling = {"tensor": z * 2 + (1 - c)}

    def copy(src, dst, ss, rs, dev):
        return pltpu.make_async_remote_copy(
            src_ref=src, dst_ref=dst, send_sem=ss, recv_sem=rs, device_id=dev, device_id_type=MESH
        )

    fetch = [
        pltpu.make_async_copy(src, dst, in_sem.at[n])
        for n, (src, dst) in enumerate([
            (og_hbm, og), (w_hbm.at[:, pl.ds(pl.multiple_of(y * 16, 16), 16), :], slab), (hb_hbm, hb),
            (live_hbm, live), (rc_hbm, rc), (gate_hbm, gate), (up_hbm, up),
        ])
    ]
    for cp in fetch:
        cp.start()

    barrier = pltpu.get_barrier_semaphore()

    def greet(s, carry):
        pl.semaphore_signal(barrier, inc=1, device_id={"tensor": lax.rem(t + s, NT)}, device_id_type=MESH)
        return carry

    lax.fori_loop(1, NT, greet, 0)
    for k in (1, 2, 3):
        pl.semaphore_signal(barrier, inc=1, device_id=xdev(k), device_id_type=MESH)
    for k in (1, -1):
        pl.semaphore_signal(barrier, inc=1, device_id=ydev(k), device_id_type=MESH)
    pend = []

    fetch[0].wait()
    og_all[2 * t] = og[:, :B]
    og_all[2 * t + 1] = og[:, B:]
    pl.semaphore_wait(barrier, NT - 1 + 3 + 2)

    def zslot(k, cc, h):
        return 2 * (lax.rem(z + k + NZ, NZ) * 2 + cc) + h

    def chunks(s):
        if s < RZ:
            return [(0, 0), (1, 1), (0, 1), (1, 0)]
        return [(0, 0), (1, 1)]

    def z_copy(s, k, e, h):
        sg = 1 if e == 0 else -1
        slot = og_all.at[zslot(-sg * s, c, h)]
        return copy(slot, slot, z_send.at[e, s + k - 1, h], z_recv.at[e, s + k - 1, h], zdev(sg * k))

    def z_start(s, e, h, ks=(2, 1)):
        for k in ks:
            if (e, h) in chunks(s + k):
                cp = z_copy(s, k, e, h)
                cp.start()
                pend.append(cp)

    def sib_start(s, e, h):
        sg = 1 if e == 0 else -1
        slot = og_all.at[zslot(-sg * s, c, h)]
        cp = copy(slot, slot, s_send.at[e, s, h], s_recv.at[e, s, h], sibling)
        cp.start()
        pend.append(cp)

    def sib_wait(s, e, h):
        sg = 1 if e == 0 else -1
        slot = og_all.at[zslot(-sg * s, 1 - c, h)]
        copy(slot, slot, s_send.at[e, s, h], s_recv.at[e, s, h], sibling).wait_recv()

    def z_step(s):
        for e, h in chunks(s):
            sg = 1 if e == 0 else -1
            slot = og_all.at[zslot(-sg * s, c, h)]
            copy(slot, slot, z_send.at[e, s - 1, h], z_recv.at[e, s - 1, h], zdev(sg)).wait_recv()
            if s in (2, 4):
                z_start(s, e, h)
            sib_start(s, e, h)

    for k in (2, 1):
        for e, h in chunks(1):
            z_start(0, e, h, (k,))
    for h in (0, 1):
        sib_start(0, 0, h)

    for cp in fetch[1:5]:
        cp.wait()
    r_out = lax.broadcasted_iota(jnp.int32, (64, 192), 0)
    r_in = lax.broadcasted_iota(jnp.int32, (64, 192), 1)
    q = lax.rem(r_out, 16)
    pick = (
        (lax.div(r_out, 16) == lax.div(r_in, 48))
        & (lax.div(q, 4) == lax.div(lax.rem(r_in, 48), 16))
        & (q < 12)
        & (x * 4 + lax.rem(q, 4) == lax.rem(r_in, 16))
    )
    pick = jnp.where(pick, 1.0, 0.0).astype(BF)
    row16 = lax.broadcasted_iota(jnp.int32, (16, B), 0)

    def make_msg(m, carry):
        rows = slab[pl.ds(m * 12, 12)].reshape(192, B)
        picked = jnp.dot(pick, rows, preferred_element_type=F32)
        for u in range(4):
            o = m * 4 + u
            tile = picked[16 * u : 16 * u + 16]
            for s in range(3):
                key = (hb[0, o * 3 + s] - o * ROWS) * 48 + hb[1, o * 3 + s]
                key = jnp.where(s < live[o], key, -1).astype(F32)
                tile = jnp.where(row16 == 12 + s, key, tile)
            msg[o] = tile.astype(BF)
        return carry

    lax.fori_loop(0, NT // 4, make_msg, 0)
    recv[t] = msg[t]

    def a_copy(s):
        o = lax.rem(t + s, NT)
        return copy(msg.at[o], recv.at[t], a_send.at[s], a_recv.at[t], {"tensor": o})

    def a_start(s, carry):
        a_copy(s).start()
        return carry

    lax.fori_loop(1, NT, a_start, 0)

    for cp in fetch[5:]:
        cp.wait()
    for i in range(ROWS):
        g = gate[:, i * B : (i + 1) * B].astype(F32)
        u = up[:, i * B : (i + 1) * B].astype(F32)
        sig = 1.0 / (1.0 + jnp.exp(-g))
        a = g * sig
        act[:, i * B : (i + 1) * B] = a
        slope_up[:, i * B : (i + 1) * B] = u * (sig * (1.0 + g * (1.0 - sig)))
        hid_t[i] = (a * u).T.astype(BF)

    lane = lax.broadcasted_iota(jnp.int32, (8, 2 * B), 1)
    block_of = lax.div(lane, 4)
    keycol = jnp.full((8, 2 * B), -100.0, F32)
    for n in range(ROWS * KEEP):
        v = ((n // KEEP) * 48 + rc[n // KEEP, n % KEEP]) * 4
        keycol = jnp.where(block_of == n, v.astype(F32), keycol)
    keycol = (keycol + lax.rem(lane, 4).astype(F32))[0:1]

    z_step(2)
    z_step(1)

    def a_wait(s, carry):
        h = lax.rem(t + s, NT)
        copy(msg.at[h], recv.at[h], a_send.at[s], a_recv.at[h], {"tensor": h}).wait_recv()
        return carry

    lax.fori_loop(1, NT, a_wait, 0)

    got = recv[...]
    gotf = got.astype(F32)
    rr = lax.broadcasted_iota(jnp.int32, (NT, 16, B), 1)
    keyrow = jnp.where(
        rr < 4, gotf[:, 12:13, :], jnp.where(rr < 8, gotf[:, 13:14, :], jnp.where(rr < 12, gotf[:, 14:15, :], -1000.0))
    )
    keyrow = (keyrow * 4.0 + lax.rem(rr, 4).astype(F32)).reshape(NT * 16, B)
    got = got.reshape(NT * 16, B)
    for v in range(2):
        hot = jnp.where(keyrow == keycol[:, v * B : (v + 1) * B], 1.0, 0.0).astype(BF)
        res = lax.dot_general(hot, got, (((0,), (0,)), ((), ())), preferred_element_type=F32).astype(BF)
        n_tiles = 8 if v == 0 else 7
        comm_x[x, 8 * v : 8 * v + n_tiles] = res[: 16 * n_tiles].reshape(n_tiles, 16, B)

    for k in (1, 3, 2):
        cp = copy(comm_x.at[x], comm_x.at[x], gx_send.at[k - 1], gx_recv.at[k - 1], xdev(k))
        cp.start()
        pend.append(cp)

    z_step(4)
    z_step(3)

    for k in (1, 3, 2):
        src = comm_x.at[lax.rem(x - k + NX, NX)]
        copy(src, src, gx_send.at[k - 1], gx_recv.at[k - 1], xdev(k)).wait_recv()
    p_out = lax.broadcasted_iota(jnp.int32, (64, 64), 0)
    p_in = lax.broadcasted_iota(jnp.int32, (64, 64), 1)
    swap = (
        (lax.div(p_out, 16) == lax.rem(lax.div(p_in, 4), 4))
        & (lax.rem(lax.div(p_out, 4), 4) == lax.div(p_in, 16))
        & (lax.rem(p_out, 4) == lax.rem(p_in, 4))
    )
    swap = jnp.where(swap, 1.0, 0.0).astype(BF)
    for g in range(15):
        res = jnp.dot(swap, comm_x[:, g].reshape(64, B), preferred_element_type=F32).astype(BF)
        for u in range(4):
            n = 4 * g + u
            i, k = n // KEEP, n % KEEP
            w_all[y, k // 6, i, :, (k % 6) * B : (k % 6 + 1) * B] = res[16 * u : 16 * u + 16]

    def y_chunks(s):
        if s < RY:
            return [(0, 0), (1, 1), (0, 1), (1, 0)]
        return [(0, 0), (1, 1)]

    def gy_slot(k, h):
        return w_all.at[lax.rem(y + k + NY, NY), h]

    def gy_start(s, e, h):
        sg = 1 if e == 0 else -1
        slot = gy_slot(-sg * (s - 1), h)
        cp = copy(slot, slot, gy_send.at[e, s - 1, h], gy_recv.at[e, s - 1, h], ydev(sg))
        cp.start()
        pend.append(cp)

    def gy_step(s):
        for e, h in y_chunks(s):
            sg = 1 if e == 0 else -1
            slot = gy_slot(-sg * s, h)
            copy(slot, slot, gy_send.at[e, s - 1, h], gy_recv.at[e, s - 1, h], ydev(sg)).wait_recv()
            if s < RY and (e, h) in y_chunks(s + 1):
                gy_start(s + 1, e, h)

    for e, h in y_chunks(1):
        gy_start(1, e, h)

    z_step(5)
    z_step(6)
    for h in (0, 1):
        sib_wait(0, 0, h)
    for s in range(1, RZ + 1):
        for e, h in chunks(s):
            sib_wait(s, e, h)

    def products(h):
        def one(i, carry):
            for p in range(3):
                k = h * 6 + 2 * p
                pair = jnp.concatenate([og_all[rc[i, k]], og_all[rc[i, k + 1]]], axis=1)
                res = jnp.dot(hid_t[i], pair, preferred_element_type=F32).astype(BF)
                part[:, h, i, :, p * 256 : (p + 1) * 256] = res.reshape(NX, 32, 256)
            return carry

        lax.fori_loop(0, ROWS, one, 0)

    def xi(k):
        return lax.rem(x + k + NX, NX)

    def rx(e, j, src, dst):
        return copy(src, dst, rx_send.at[e, j], rx_recv.at[e, j], xdev(1 if e == 0 else -1))

    def rx_start(*args):
        cp = rx(*args)
        cp.start()
        pend.append(cp)

    products(0)
    rx_start(0, 0, part.at[xi(2), 0], buf_x.at[0])
    rx_start(1, 1, part.at[xi(-1), 0], fin_x.at[1, 0])
    products(1)
    rx_start(1, 0, part.at[xi(2), 1], buf_x.at[1])
    rx_start(0, 1, part.at[xi(1), 1], fin_x.at[0, 1])
    gy_step(1)
    for e in (0, 1):
        rx(e, 0, part.at[xi(2), e], buf_x.at[e]).wait_recv()
        mine = part[xi(1 if e == 0 else -1), e].astype(F32)
        snd_x[e] = (mine + buf_x[e].astype(F32)).astype(BF)
        rx_start(e, 2, snd_x.at[e], fin_x.at[e, e])
    gy_step(2)
    gy_step(3)
    gy_step(4)

    def hidden_grad(i, carry):
        total = jnp.zeros((B, B), F32)
        for h in range(2):
            left = jnp.concatenate([og_all[rc[i, h * 6 + k]] for k in range(6)], axis=1)
            right = w_all[:, h, i].reshape(B, HALF)
            total = total + lax.dot_general(
                left, right, (((1,), (1,)), ((), ())), preferred_element_type=F32
            )
        cols = pl.ds(pl.multiple_of(i * B, B), B)
        gg[:, cols] = (total * slope_up[:, cols]).astype(BF)
        ug[:, cols] = (total * act[:, cols]).astype(BF)
        return carry

    lax.fori_loop(0, ROWS, hidden_grad, 0)
    gg_out = pltpu.make_async_copy(gg, gg_hbm, out_sem.at[0])
    gg_out.start()
    ug_out = pltpu.make_async_copy(ug, ug_hbm, out_sem.at[1])
    ug_out.start()

    for e in (0, 1):
        rx(e, 1, part.at[xi(1), 1 - e], fin_x.at[e, 1 - e]).wait_recv()
        rx(e, 2, snd_x.at[e], fin_x.at[e, e]).wait_recv()
    low = lax.broadcasted_iota(jnp.int32, (4, 8, B), 1) < 4
    for h in range(2):
        for i in range(ROWS):
            own = part[x, h, i].astype(F32) + fin_x[0, h, i].astype(F32) + fin_x[1, h, i].astype(F32)
            own = own.reshape(4, 8, HALF)
            for p in range(3):
                a0 = own[:, :, 2 * p * B : (2 * p + 1) * B]
                a1 = own[:, :, (2 * p + 1) * B : (2 * p + 2) * B]
                d0 = jnp.where(low, a0, pltpu.roll(a1, 4, 1))
                d1 = jnp.where(low, pltpu.roll(a0, 4, 1), a1)
                first = (i * KEEP + h * 6 + 2 * p) * 4
                yin[:, 0, first : first + 8, :] = d0
                yin[:, 1, first : first + 8, :] = d1

    span = [pl.ds(0, CUT), pl.ds(CUT, NROW - CUT)]

    def yblock(k, h):
        yy = lax.rem(y + k + NY, NY)
        return yin[lax.div(yy, 2), lax.rem(yy, 2), span[h], :]

    def ry(s, e, h):
        return copy(
            snd_y.at[e, s - 1, span[h], :], rcv_y.at[e, s - 1, span[h], :],
            ry_send.at[e, s - 1, h], ry_recv.at[e, s - 1, h], ydev(1 if e == 0 else -1),
        )

    for s in range(1, RY + 1):
        for e, h in ([(0, 0), (1, 1)] if s == 1 else [(0, 1), (1, 0), (0, 0), (1, 1)] if s == 2 else [(0, 0), (1, 1), (0, 1), (1, 0)]):
            sg = 1 if e == 0 else -1
            v = yblock(sg * (RY + 1 - s), h)
            if s > 2 or (s == 2 and e == h):
                ry(s - 1, e, h).wait_recv()
                v = v + rcv_y[e, s - 2, span[h], :].astype(F32)
            snd_y[e, s - 1, span[h], :] = v.astype(BF)
            cp = ry(s, e, h)
            cp.start()
            pend.append(cp)
    for h in (0, 1):
        for e in (0, 1):
            ry(RY, e, h).wait_recv()
        v = yblock(0, h) + rcv_y[0, RY - 1, span[h], :].astype(F32) + rcv_y[1, RY - 1, span[h], :].astype(F32)
        wg[span[h], :] = v.astype(BF)

    wg_out = pltpu.make_async_copy(wg, wg_hbm, out_sem.at[2])
    wg_out.start()

    def a_done(s, carry):
        a_copy(s).wait_send()
        return carry

    lax.fori_loop(1, NT, a_done, 0)
    for cp in pend:
        cp.wait_send()
    for cp in (gg_out, ug_out, wg_out):
        cp.wait()


def local(gate_pre, up_pre, out_grad, weight_slots, holder_blocks, holder_live_slots, row_columns):
    hbm = pl.BlockSpec(memory_space=pl.ANY)
    dma = pltpu.SemaphoreType.DMA
    gate_grad, up_grad, weight_grad = pl.pallas_call(
        kernel,
        out_shape=(
            jax.ShapeDtypeStruct(gate_pre.shape, BF),
            jax.ShapeDtypeStruct(gate_pre.shape, BF),
            jax.ShapeDtypeStruct((NROW, B), BF),
        ),
        in_specs=[hbm] * 7,
        out_specs=(hbm, hbm, hbm),
        scratch_shapes=[
            pltpu.VMEM(gate_pre.shape, BF), pltpu.VMEM(up_pre.shape, BF), pltpu.VMEM(out_grad.shape, BF),
            pltpu.SMEM((2, 3 * NT), jnp.int32), pltpu.SMEM((NT,), jnp.int32), pltpu.SMEM((ROWS, KEEP), jnp.int32),
            pltpu.VMEM(gate_pre.shape, BF), pltpu.VMEM(gate_pre.shape, BF), pltpu.VMEM((NROW, B), BF),
            pltpu.VMEM((2 * NT, B, B), BF),
            pltpu.VMEM((3 * NT, 16, B), BF),
            pltpu.VMEM((NT, 16, B), BF),
            pltpu.VMEM((NT, 16, B), BF),
            pltpu.VMEM((NX, 15, 16, B), BF),
            pltpu.VMEM((NY, 2, ROWS, 16, HALF), BF),
            pltpu.VMEM((B, ROWS * B), F32),
            pltpu.VMEM((B, ROWS * B), F32),
            pltpu.VMEM((ROWS, B, B), BF),
            pltpu.VMEM((NX, 2, ROWS, 32, HALF), BF),
            pltpu.VMEM((2, ROWS, 32, HALF), BF),
            pltpu.VMEM((2, 2, ROWS, 32, HALF), BF),
            pltpu.VMEM((2, ROWS, 32, HALF), BF),
            pltpu.VMEM((NY // 2, 2, NROW, B), F32),
            pltpu.VMEM((2, RY, NROW, B), BF),
            pltpu.VMEM((2, RY, NROW, B), BF),
            dma((7,)), dma((3,)),
            dma((2, RZ, 2)), dma((2, RZ, 2)),
            dma((2, RZ + 1, 2)), dma((2, RZ + 1, 2)),
            dma((NT,)), dma((NT,)),
            dma((3,)), dma((3,)),
            dma((2, RY, 2)), dma((2, RY, 2)),
            dma((2, 3)), dma((2, 3)),
            dma((2, RY, 2)), dma((2, RY, 2)),
        ],
        compiler_params=pltpu.CompilerParams(
            collective_id=0, has_side_effects=True, vmem_limit_bytes=62 * 1024 * 1024
        ),
        cost_estimate=pl.CostEstimate(flops=600_000_000, bytes_accessed=4_000_000, transcendentals=82_000),
    )(gate_pre, up_pre, out_grad, weight_slots, holder_blocks.T, holder_live_slots, row_columns)
    return gate_grad, up_grad, weight_grad.reshape(ROWS * KEEP, 4 * B)


def solution(mesh):
    placed = (
        P("dp", "tensor"),
        P("dp", "tensor"),
        P("dp", "tensor"),
        P("tensor", None, None),
        P("tensor", None),
        P("tensor"),
        P("tensor", None),
    )
    return jax.shard_map(
        local,
        mesh=mesh,
        in_specs=placed,
        out_specs=(P("dp", "tensor"), P("dp", "tensor"), P("tensor", "dp")),
        check_vma=False,
    )
```

```python
import jax
import jax.numpy as jnp
from jax import lax
from jax.experimental import pallas as pl
from jax.experimental.pallas import tpu as pltpu
from jax.sharding import PartitionSpec as P

MESH = pl.DeviceIdType.MESH
NX, NY, NZ = 4, 8, 12
NT = 2 * NZ
RZ, RY = NZ // 2, NY // 2
ROWS, KEEP, B = 5, 12, 128
HALF = KEEP // 2
TRI = 3 * B
BF, F32 = jnp.bfloat16, jnp.float32
NROW = ROWS * KEEP * 4
HROW = NROW // 2


def kernel(
    gate_hbm, up_hbm, og_hbm, w_hbm, hb_hbm, live_hbm, rc_hbm,
    gg_hbm, ug_hbm, wg_hbm,
    gate, up, og, hb, live, rc, gg, ug, wg,
    og_all, slab, msg, recv, comm_y, w_all, act, slope_up, hid_t, part_a, part_b,
    buf_x, fin_x, snd_x, far_y, near_y, one_y, two_y, snd_two, yin, snd_ya, rcv_ya, xin, snd_xb, rcv_xb, wgf,
    in_sem, out_sem, z_send, z_recv, s_send, s_recv, a_send, a_recv, gy_send, gy_recv, gx_send, gx_recv,
    rx_send, rx_recv, far_send, far_recv, near_send, near_recv, one_send, one_recv, two_send, two_recv,
    ya_send, ya_recv, xb_send, xb_recv,
):
    t, d = lax.axis_index("tensor"), lax.axis_index("dp")
    z, c = lax.div(t, 2), lax.rem(t, 2)
    x, y = lax.div(d, NY), lax.rem(d, NY)

    def zdev(k):
        return {"tensor": lax.rem(z + k + NZ, NZ) * 2 + c}

    def xdev(k):
        return {"dp": lax.rem(x + k + NX, NX) * NY + y}

    def ydev(k):
        return {"dp": x * NY + lax.rem(y + k + NY, NY)}

    sibling = {"tensor": z * 2 + (1 - c)}

    def copy(src, dst, ss, rs, dev):
        return pltpu.make_async_remote_copy(
            src_ref=src, dst_ref=dst, send_sem=ss, recv_sem=rs, device_id=dev, device_id_type=MESH
        )

    fetch = [
        pltpu.make_async_copy(src, dst, in_sem.at[n])
        for n, (src, dst) in enumerate([
            (og_hbm, og), (w_hbm.at[:, pl.ds(pl.multiple_of(x * 32 + lax.div(y, 4) * 16, 16), 16), :], slab), (hb_hbm, hb),
            (live_hbm, live), (rc_hbm, rc), (gate_hbm, gate), (up_hbm, up),
        ])
    ]
    for cp in fetch:
        cp.start()

    barrier = pltpu.get_barrier_semaphore()

    def greet(s, carry):
        pl.semaphore_signal(barrier, inc=1, device_id={"tensor": lax.rem(t + s, NT)}, device_id_type=MESH)
        return carry

    lax.fori_loop(1, NT, greet, 0)
    for k in (1, 2, 3):
        pl.semaphore_signal(barrier, inc=1, device_id=xdev(k), device_id_type=MESH)
    for k in range(1, NY):
        pl.semaphore_signal(barrier, inc=1, device_id=ydev(k), device_id_type=MESH)
    pend = []

    fetch[0].wait()
    og_all[2 * t] = og[:, :B]
    og_all[2 * t + 1] = og[:, B:]
    pl.semaphore_wait(barrier, NT - 1 + NX - 1 + NY - 1)

    def zslot(k, cc, h):
        return 2 * (lax.rem(z + k + NZ, NZ) * 2 + cc) + h

    class Ring:
        def __init__(self, radius, slot, dev, send, recv):
            self.radius, self.slot, self.dev, self.send, self.recv = radius, slot, dev, send, recv

        def chunks(self, s):
            return [(0, 0), (1, 1), (0, 1), (1, 0)][: 4 if s < self.radius else 2 if s == self.radius else 0]

        def copy(self, s, k, e, h):
            sg = 1 if e == 0 else -1
            slot = self.slot(-sg * s, h)
            return copy(slot, slot, self.send.at[e, s + k - 1, h], self.recv.at[e, s + k - 1, h], self.dev(sg * k))

        def start(self, s, e, h, ks=(2, 1)):
            for k in ks:
                if (e, h) in self.chunks(s + k):
                    cp = self.copy(s, k, e, h)
                    cp.start()
                    pend.append(cp)

        def open(self):
            for k in (2, 1):
                for e, h in self.chunks(1):
                    self.start(0, e, h, (k,))

        def step(self, s, arrived=None):
            for e, h in self.chunks(s):
                sg = 1 if e == 0 else -1
                slot = self.slot(-sg * s, h)
                copy(slot, slot, self.send.at[e, s - 1, h], self.recv.at[e, s - 1, h], self.dev(sg)).wait_recv()
                if s % 2 == 0:
                    self.start(s, e, h)
                if arrived is not None:
                    arrived(s, e, h)

    z_ring = Ring(RZ, lambda k, h: og_all.at[zslot(k, c, h)], zdev, z_send, z_recv)

    def sib_start(s, e, h):
        sg = 1 if e == 0 else -1
        slot = og_all.at[zslot(-sg * s, c, h)]
        cp = copy(slot, slot, s_send.at[e, s, h], s_recv.at[e, s, h], sibling)
        cp.start()
        pend.append(cp)

    def sib_wait(s, e, h):
        sg = 1 if e == 0 else -1
        slot = og_all.at[zslot(-sg * s, 1 - c, h)]
        copy(slot, slot, s_send.at[e, s, h], s_recv.at[e, s, h], sibling).wait_recv()

    def z_step(s):
        z_ring.step(s, sib_start)

    z_ring.open()
    for h in (0, 1):
        sib_start(0, 0, h)

    for cp in fetch[1:5]:
        cp.wait()
    r_out = lax.broadcasted_iota(jnp.int32, (64, 192), 0)
    r_in = lax.broadcasted_iota(jnp.int32, (64, 192), 1)
    q = lax.rem(r_out, 16)
    pick = (
        (lax.div(r_out, 16) == lax.div(r_in, 48))
        & (lax.div(q, 4) == lax.div(lax.rem(r_in, 48), 16))
        & (q < 12)
        & (lax.rem(y, 4) * 4 + lax.rem(q, 4) == lax.rem(r_in, 16))
    )
    pick = jnp.where(pick, 1.0, 0.0).astype(BF)
    row16 = lax.broadcasted_iota(jnp.int32, (16, B), 0)

    def make_msg(m, carry):
        rows = slab[pl.ds(m * 12, 12)].reshape(192, B)
        picked = jnp.dot(pick, rows, preferred_element_type=F32)
        for u in range(4):
            o = m * 4 + u
            tile = picked[16 * u : 16 * u + 16]
            for s in range(3):
                key = (hb[0, o * 3 + s] - o * ROWS) * 48 + hb[1, o * 3 + s]
                key = jnp.where(s < live[o], key, -1).astype(F32)
                tile = jnp.where(row16 == 12 + s, key, tile)
            msg[o] = tile.astype(BF)
        return carry

    lax.fori_loop(0, NT // 4, make_msg, 0)
    recv[t] = msg[t]

    def a_copy(s):
        o = lax.rem(t + s, NT)
        return copy(msg.at[o], recv.at[t], a_send.at[s], a_recv.at[t], {"tensor": o})

    def a_start(s, carry):
        a_copy(s).start()
        return carry

    lax.fori_loop(1, NT, a_start, 0)

    for cp in fetch[5:]:
        cp.wait()
    o_row = lax.broadcasted_iota(jnp.int32, (B, B), 0)
    o_col = lax.broadcasted_iota(jnp.int32, (B, B), 1)
    to_y = (
        (lax.div(o_row, 16) == lax.rem(lax.div(o_col, 4), NY))
        & (lax.rem(lax.div(o_row, 4), NX) == lax.div(o_col, 32))
        & (lax.rem(o_row, 4) == lax.rem(o_col, 4))
    )
    to_y = jnp.where(to_y, 1.0, 0.0).astype(BF)
    for i in range(ROWS):
        g = gate[:, i * B : (i + 1) * B].astype(F32)
        u = up[:, i * B : (i + 1) * B].astype(F32)
        sig = 1.0 / (1.0 + jnp.exp(-g))
        a = g * sig
        act[:, i * B : (i + 1) * B] = a
        slope_up[:, i * B : (i + 1) * B] = u * (sig * (1.0 + g * (1.0 - sig)))
        hid = (a * u).T.astype(BF)
        hid_t[0, i] = hid
        hid_t[1, i] = jnp.dot(to_y, hid, preferred_element_type=F32).astype(BF)

    lane = lax.broadcasted_iota(jnp.int32, (8, 2 * B), 1)
    block_of = lax.div(lane, 4)
    keycol = jnp.full((8, 2 * B), -100.0, F32)
    for n in range(ROWS * KEEP):
        v = ((n // KEEP) * 48 + rc[n // KEEP, n % KEEP]) * 4
        keycol = jnp.where(block_of == n, v.astype(F32), keycol)
    keycol = (keycol + lax.rem(lane, 4).astype(F32))[0:1]

    z_step(2)
    z_step(1)

    def a_wait(s, carry):
        h = lax.rem(t + s, NT)
        copy(msg.at[h], recv.at[h], a_send.at[s], a_recv.at[h], {"tensor": h}).wait_recv()
        return carry

    lax.fori_loop(1, NT, a_wait, 0)

    got = recv[...]
    gotf = got.astype(F32)
    rr = lax.broadcasted_iota(jnp.int32, (NT, 16, B), 1)
    keyrow = jnp.where(
        rr < 4, gotf[:, 12:13, :], jnp.where(rr < 8, gotf[:, 13:14, :], jnp.where(rr < 12, gotf[:, 14:15, :], -1000.0))
    )
    keyrow = (keyrow * 4.0 + lax.rem(rr, 4).astype(F32)).reshape(NT * 16, B)
    got = got.reshape(NT * 16, B)
    for v in range(2):
        hot = jnp.where(keyrow == keycol[:, v * B : (v + 1) * B], 1.0, 0.0).astype(BF)
        res = lax.dot_general(hot, got, (((0,), (0,)), ((), ())), preferred_element_type=F32).astype(BF)
        n_tiles = 8 if v == 0 else 7
        comm_y[y, 8 * v : 8 * v + n_tiles] = res[: 16 * n_tiles].reshape(n_tiles, 16, B)

    y_ring = Ring(
        RY,
        lambda k, h: comm_y.at[lax.rem(y + k + NY, NY), pl.ds(8 * h, 8 - h)],
        ydev, gy_send, gy_recv,
    )
    y_ring.open()

    z_step(4)
    z_step(3)
    y_ring.step(2)
    z_step(6)
    z_step(5)
    for h in (0, 1):
        sib_wait(0, 0, h)
    for s in range(1, RZ + 1):
        for e, h in z_ring.chunks(s):
            sib_wait(s, e, h)

    def products(half):
        def one(i, carry):
            for p in range(2):
                k = half * HALF + 3 * p
                three = jnp.concatenate([og_all[rc[i, k + m]] for m in range(3)], axis=1)
                res = jnp.dot(hid_t[half, i], three, preferred_element_type=F32).astype(BF)
                if half == 0:
                    part_a[:, p, i] = res.reshape(NX, 32, TRI)
                else:
                    part_b[:, p, i] = res.reshape(NY, 16, TRI)
            return carry

        lax.fori_loop(0, ROWS, one, 0)

    def xi(k):
        return lax.rem(x + k + NX, NX)

    def yi(k):
        return lax.rem(y + k + NY, NY)

    def rx(e, j, src, dst):
        return copy(src, dst, rx_send.at[e, j], rx_recv.at[e, j], xdev(1 if e == 0 else -1))

    def begin(cp):
        cp.start()
        pend.append(cp)

    def far(e):
        sg = 1 if e == 0 else -1
        return copy(part_b.at[yi(4), e], far_y.at[e], far_send.at[e], far_recv.at[e], ydev(2 * sg))

    def near(e, p):
        sg = 1 if e == 0 else -1
        return copy(part_b.at[yi(3 * sg), p], near_y.at[e, p], near_send.at[e, p], near_recv.at[e, p], ydev(sg))

    def one_hop(e, p):
        sg = 1 if e == 0 else -1
        return copy(part_b.at[yi(sg), p], one_y.at[e, p], one_send.at[e, p], one_recv.at[e, p], ydev(sg))

    def two_hops(e, p):
        sg = 1 if e == 0 else -1
        return copy(snd_two.at[e, p], two_y.at[e, p], two_send.at[e, p], two_recv.at[e, p], ydev(2 * sg))

    products(1)
    for e in (0, 1):
        begin(far(e))
    for p in (0, 1):
        for e in (0, 1):
            begin(near(e, e if p == 0 else 1 - e))
    products(0)
    begin(rx(0, 0, part_a.at[xi(2), 0], buf_x.at[0]))
    begin(rx(1, 0, part_a.at[xi(2), 1], buf_x.at[1]))
    begin(rx(0, 1, part_a.at[xi(1), 1], fin_x.at[0, 1]))
    begin(rx(1, 1, part_a.at[xi(-1), 0], fin_x.at[1, 0]))
    for p in (0, 1):
        for e in (0, 1):
            begin(one_hop(e, p))

    y_ring.step(1)
    y_ring.step(3)
    y_ring.step(4)
    swap = (
        (lax.div(o_row, 32) == lax.rem(lax.div(o_col, 4), 4))
        & (lax.rem(lax.div(o_row, 4), NY) == lax.div(o_col, 16))
        & (lax.rem(o_row, 4) == lax.rem(o_col, 4))
    )
    swap = jnp.where(swap, 1.0, 0.0).astype(BF)
    for g in range(15):
        res = jnp.dot(swap, comm_y[:, g].reshape(B, B), preferred_element_type=F32).astype(BF)
        for u in range(4):
            n = 4 * g + u
            i, k = n // KEEP, n % KEEP
            w_all[x, k // 3, i, :, (k % 3) * B : (k % 3 + 1) * B] = res[32 * u : 32 * u + 32]

    def gx(s, e, q, back):
        sg = 1 if e == 0 else -1
        slot = w_all.at[xi(-sg * back), q]
        return copy(slot, slot, gx_send.at[e, s - 1, q], gx_recv.at[e, s - 1, q], xdev(sg))

    x_all = [(0, 0), (1, 2), (0, 1), (1, 3), (0, 2), (1, 0), (0, 3), (1, 1)]
    for e, q in x_all:
        begin(gx(1, e, q, 0))

    for p in (0, 1):
        for e in (0, 1):
            q = 1 - e if p == 0 else e
            near(e, q).wait_recv()
            sg = 1 if e == 0 else -1
            v = part_b[yi(2 * sg), q].astype(F32) + near_y[e, q].astype(F32)
            if q == e:
                far(e).wait_recv()
                v = v + far_y[e].astype(F32)
            snd_two[e, q] = v.astype(BF)
            begin(two_hops(e, q))
    for e in (0, 1):
        rx(e, 0, part_a.at[xi(2), e], buf_x.at[e]).wait_recv()
        v = part_a[xi(1 if e == 0 else -1), e].astype(F32) + buf_x[e].astype(F32)
        snd_x[e] = v.astype(BF)
        begin(rx(e, 2, snd_x.at[e], fin_x.at[e, e]))

    for e, q in x_all:
        gx(1, e, q, 1).wait_recv()
        if (e, q) in x_all[:4]:
            begin(gx(2, e, q, 1))

    def scatter(own, groups, dst, i):
        low = lax.broadcasted_iota(jnp.int32, (groups, 8, B), 1) < 4
        own = own.reshape(groups, 8, HALF * B)
        for p in range(HALF // 2):
            a0 = own[:, :, 2 * p * B : (2 * p + 1) * B]
            a1 = own[:, :, (2 * p + 1) * B : (2 * p + 2) * B]
            first = (i * HALF + 2 * p) * 4
            dst[:, 0, first : first + 8, :] = jnp.where(low, a0, pltpu.roll(a1, 4, 1))
            dst[:, 1, first : first + 8, :] = jnp.where(low, pltpu.roll(a0, 4, 1), a1)

    for e in (0, 1):
        rx(e, 1, part_a.at[xi(1), 1 - e], fin_x.at[e, 1 - e]).wait_recv()
        rx(e, 2, snd_x.at[e], fin_x.at[e, e]).wait_recv()
    yin[:, :, HROW:, :] = jnp.zeros((NY // 2, 2, B - HROW, B), F32)
    for i in range(ROWS):
        own = [
            part_a[x, p, i].astype(F32) + fin_x[0, p, i].astype(F32) + fin_x[1, p, i].astype(F32) for p in (0, 1)
        ]
        scatter(jnp.concatenate(own, axis=1), NY // 2, yin, i)
    snd_ya[...] = yin[...].reshape(NY, B, B).astype(BF)

    def ya(k):
        return copy(snd_ya.at[yi(k)], rcv_ya.at[k - 1], ya_send.at[k - 1], ya_recv.at[k - 1], ydev(k))

    for k in (4, 3, 5, 2, 6, 1, 7):
        begin(ya(k))

    for e in (0, 1):
        for p in (0, 1):
            one_hop(e, p).wait_recv()
            two_hops(e, p).wait_recv()
    xin[:, :, HROW:, :] = jnp.zeros((NX // 2, 2, B - HROW, B), F32)
    for i in range(ROWS):
        own = [
            part_b[y, p, i].astype(F32) + one_y[0, p, i].astype(F32) + one_y[1, p, i].astype(F32)
            + two_y[0, p, i].astype(F32) + two_y[1, p, i].astype(F32)
            for p in (0, 1)
        ]
        scatter(jnp.concatenate(own, axis=1), NX // 2, xin, i)
    snd_xb[...] = xin[...].reshape(NX, B, B).astype(BF)

    def xb(k):
        return copy(snd_xb.at[xi(k)], rcv_xb.at[k - 1], xb_send.at[k - 1], xb_recv.at[k - 1], xdev(k))

    for k in (2, 1, 3):
        begin(xb(k))

    for e, q in x_all[:4]:
        gx(2, e, q, 2).wait_recv()

    def hidden_grad(i, carry):
        total = jnp.zeros((B, B), F32)
        for q in range(4):
            left = jnp.concatenate([og_all[rc[i, q * 3 + m]] for m in range(3)], axis=1)
            right = w_all[:, q, i].reshape(B, TRI)
            total = total + lax.dot_general(left, right, (((1,), (1,)), ((), ())), preferred_element_type=F32)
        cols = pl.ds(pl.multiple_of(i * B, B), B)
        gg[:, cols] = (total * slope_up[:, cols]).astype(BF)
        ug[:, cols] = (total * act[:, cols]).astype(BF)
        return carry

    lax.fori_loop(0, ROWS, hidden_grad, 0)
    gg_out = pltpu.make_async_copy(gg, gg_hbm, out_sem.at[0])
    gg_out.start()
    ug_out = pltpu.make_async_copy(ug, ug_hbm, out_sem.at[1])
    ug_out.start()

    for half, n, mine, box, cps in (
        (0, NY, yin[lax.div(y, 2), lax.rem(y, 2)], rcv_ya, ya),
        (1, NX, xin[lax.div(x, 2), lax.rem(x, 2)], rcv_xb, xb),
    ):
        for k in range(1, n):
            cps(k).wait_recv()
            mine = mine + box[k - 1].astype(F32)
        for i in range(ROWS):
            first = (i * KEEP + half * HALF) * 4
            wgf[first : first + 4 * HALF, :] = mine[i * 4 * HALF : (i + 1) * 4 * HALF]
    wg[...] = wgf[...].astype(BF)
    wg_out = pltpu.make_async_copy(wg, wg_hbm, out_sem.at[2])
    wg_out.start()

    def a_done(s, carry):
        a_copy(s).wait_send()
        return carry

    lax.fori_loop(1, NT, a_done, 0)
    for cp in pend:
        cp.wait_send()
    for cp in (gg_out, ug_out, wg_out):
        cp.wait()


def local(gate_pre, up_pre, out_grad, weight_slots, holder_blocks, holder_live_slots, row_columns):
    hbm = pl.BlockSpec(memory_space=pl.ANY)
    dma = pltpu.SemaphoreType.DMA
    gate_grad, up_grad, weight_grad = pl.pallas_call(
        kernel,
        out_shape=(
            jax.ShapeDtypeStruct(gate_pre.shape, BF),
            jax.ShapeDtypeStruct(gate_pre.shape, BF),
            jax.ShapeDtypeStruct((NROW, B), BF),
        ),
        in_specs=[hbm] * 7,
        out_specs=(hbm, hbm, hbm),
        scratch_shapes=[
            pltpu.VMEM(gate_pre.shape, BF), pltpu.VMEM(up_pre.shape, BF), pltpu.VMEM(out_grad.shape, BF),
            pltpu.SMEM((2, 3 * NT), jnp.int32), pltpu.SMEM((NT,), jnp.int32), pltpu.SMEM((ROWS, KEEP), jnp.int32),
            pltpu.VMEM(gate_pre.shape, BF), pltpu.VMEM(gate_pre.shape, BF), pltpu.VMEM((NROW, B), BF),
            pltpu.VMEM((2 * NT, B, B), BF),
            pltpu.VMEM((3 * NT, 16, B), BF),
            pltpu.VMEM((NT, 16, B), BF),
            pltpu.VMEM((NT, 16, B), BF),
            pltpu.VMEM((NY, 15, 16, B), BF),
            pltpu.VMEM((NX, 4, ROWS, 32, TRI), BF),
            pltpu.VMEM((B, ROWS * B), F32),
            pltpu.VMEM((B, ROWS * B), F32),
            pltpu.VMEM((2, ROWS, B, B), BF),
            pltpu.VMEM((NX, 2, ROWS, 32, TRI), BF),
            pltpu.VMEM((NY, 2, ROWS, 16, TRI), BF),
            pltpu.VMEM((2, ROWS, 32, TRI), BF),
            pltpu.VMEM((2, 2, ROWS, 32, TRI), BF),
            pltpu.VMEM((2, ROWS, 32, TRI), BF),
            pltpu.VMEM((2, ROWS, 16, TRI), BF),
            pltpu.VMEM((2, 2, ROWS, 16, TRI), BF),
            pltpu.VMEM((2, 2, ROWS, 16, TRI), BF),
            pltpu.VMEM((2, 2, ROWS, 16, TRI), BF),
            pltpu.VMEM((2, 2, ROWS, 16, TRI), BF),
            pltpu.VMEM((NY // 2, 2, B, B), F32),
            pltpu.VMEM((NY, B, B), BF), pltpu.VMEM((NY - 1, B, B), BF),
            pltpu.VMEM((NX // 2, 2, B, B), F32),
            pltpu.VMEM((NX, B, B), BF), pltpu.VMEM((NX - 1, B, B), BF),
            pltpu.VMEM((NROW, B), F32),
            dma((7,)), dma((3,)),
            dma((2, RZ, 2)), dma((2, RZ, 2)),
            dma((2, RZ + 1, 2)), dma((2, RZ + 1, 2)),
            dma((NT,)), dma((NT,)),
            dma((2, RY, 2)), dma((2, RY, 2)),
            dma((2, 2, 4)), dma((2, 2, 4)),
            dma((2, 3)), dma((2, 3)),
            dma((2,)), dma((2,)), dma((2, 2)), dma((2, 2)),
            dma((2, 2)), dma((2, 2)), dma((2, 2)), dma((2, 2)),
            dma((NY - 1,)), dma((NY - 1,)), dma((NX - 1,)), dma((NX - 1,)),
        ],
        compiler_params=pltpu.CompilerParams(
            collective_id=0, has_side_effects=True, vmem_limit_bytes=62 * 1024 * 1024
        ),
        cost_estimate=pl.CostEstimate(flops=600_000_000, bytes_accessed=4_000_000, transcendentals=82_000),
    )(gate_pre, up_pre, out_grad, weight_slots, holder_blocks.T, holder_live_slots, row_columns)
    return gate_grad, up_grad, weight_grad.reshape(ROWS * KEEP, 4 * B)


def solution(mesh):
    placed = (
        P("dp", "tensor"),
        P("dp", "tensor"),
        P("dp", "tensor"),
        P("tensor", None, None),
        P("tensor", None),
        P("tensor"),
        P("tensor", None),
    )
    return jax.shard_map(
        local,
        mesh=mesh,
        in_specs=placed,
        out_specs=(P("dp", "tensor"), P("dp", "tensor"), P("tensor", "dp")),
        check_vma=False,
    )
```

```python
import jax
import jax.numpy as jnp
from jax import lax
from jax.experimental import pallas as pl
from jax.experimental.pallas import tpu as pltpu
from jax.sharding import PartitionSpec as P

MESH = pl.DeviceIdType.MESH
NX, NY, NZ = 4, 8, 12
NT = 2 * NZ
RZ, RY = NZ // 2, NY // 2
ROWS, KEEP, B = 5, 12, 128
HALF = KEEP // 2
TRI = 3 * B
BF, F32 = jnp.bfloat16, jnp.float32
NROW = ROWS * KEEP * 4
HROW = NROW // 2


def kernel(
    gate_hbm, up_hbm, og_hbm, w_hbm, hb_hbm, live_hbm, rc_hbm,
    gg_hbm, ug_hbm, wg_hbm,
    gate, up, og, hb, live, rc, gg, ug, wg,
    og_all, slab, msg, recv, comm_y, comm_x, w_all, w_b, act, slope_up, hid_t, part_a, part_b,
    buf_x, fin_x, snd_x, far_y, near_y, one_y, two_y, snd_two, yin, snd_ya, rcv_ya, xin, snd_xb, rcv_xb, wgf,
    in_sem, out_sem, z_send, z_recv, s_send, s_recv, a_send, a_recv, gy_send, gy_recv, gx_send, gx_recv, c_send, c_recv, wy_send, wy_recv,
    rx_send, rx_recv, far_send, far_recv, near_send, near_recv, one_send, one_recv, two_send, two_recv,
    ya_send, ya_recv, xb_send, xb_recv,
):
    t, d = lax.axis_index("tensor"), lax.axis_index("dp")
    z, c = lax.div(t, 2), lax.rem(t, 2)
    x, y = lax.div(d, NY), lax.rem(d, NY)

    def zdev(k):
        return {"tensor": lax.rem(z + k + NZ, NZ) * 2 + c}

    def xdev(k):
        return {"dp": lax.rem(x + k + NX, NX) * NY + y}

    def ydev(k):
        return {"dp": x * NY + lax.rem(y + k + NY, NY)}

    sibling = {"tensor": z * 2 + (1 - c)}

    def copy(src, dst, ss, rs, dev):
        return pltpu.make_async_remote_copy(
            src_ref=src, dst_ref=dst, send_sem=ss, recv_sem=rs, device_id=dev, device_id_type=MESH
        )

    fetch = [
        pltpu.make_async_copy(src, dst, in_sem.at[n])
        for n, (src, dst) in enumerate([
            (og_hbm, og), (w_hbm.at[:, pl.ds(pl.multiple_of(x * 32 + lax.div(y, 4) * 16, 16), 16), :], slab), (hb_hbm, hb),
            (live_hbm, live), (rc_hbm, rc), (gate_hbm, gate), (up_hbm, up),
        ])
    ]
    for cp in fetch:
        cp.start()

    barrier = pltpu.get_barrier_semaphore()

    def greet(s, carry):
        pl.semaphore_signal(barrier, inc=1, device_id={"tensor": lax.rem(t + s, NT)}, device_id_type=MESH)
        return carry

    lax.fori_loop(1, NT, greet, 0)
    for k in (1, 2, 3):
        pl.semaphore_signal(barrier, inc=1, device_id=xdev(k), device_id_type=MESH)
    for k in range(1, NY):
        pl.semaphore_signal(barrier, inc=1, device_id=ydev(k), device_id_type=MESH)
    pend = []

    fetch[0].wait()
    og_all[2 * t] = og[:, :B]
    og_all[2 * t + 1] = og[:, B:]
    pl.semaphore_wait(barrier, NT - 1 + NX - 1 + NY - 1)

    def zslot(k, cc, h):
        return 2 * (lax.rem(z + k + NZ, NZ) * 2 + cc) + h

    class Ring:
        def __init__(self, radius, slot, dev, send, recv):
            self.radius, self.slot, self.dev, self.send, self.recv = radius, slot, dev, send, recv

        def chunks(self, s):
            return [(0, 0), (1, 1), (0, 1), (1, 0)][: 4 if s < self.radius else 2 if s == self.radius else 0]

        def copy(self, s, k, e, h):
            sg = 1 if e == 0 else -1
            slot = self.slot(-sg * s, h)
            return copy(slot, slot, self.send.at[e, s + k - 1, h], self.recv.at[e, s + k - 1, h], self.dev(sg * k))

        def start(self, s, e, h, ks=(2, 1)):
            for k in ks:
                if (e, h) in self.chunks(s + k):
                    cp = self.copy(s, k, e, h)
                    cp.start()
                    pend.append(cp)

        def open(self):
            for k in (2, 1):
                for e, h in self.chunks(1):
                    self.start(0, e, h, (k,))

        def step(self, s, arrived=None):
            for e, h in self.chunks(s):
                sg = 1 if e == 0 else -1
                slot = self.slot(-sg * s, h)
                copy(slot, slot, self.send.at[e, s - 1, h], self.recv.at[e, s - 1, h], self.dev(sg)).wait_recv()
                if s % 2 == 0:
                    self.start(s, e, h)
                if arrived is not None:
                    arrived(s, e, h)

    z_ring = Ring(RZ, lambda k, h: og_all.at[zslot(k, c, h)], zdev, z_send, z_recv)

    def sib_start(s, e, h):
        sg = 1 if e == 0 else -1
        slot = og_all.at[zslot(-sg * s, c, h)]
        cp = copy(slot, slot, s_send.at[e, s, h], s_recv.at[e, s, h], sibling)
        cp.start()
        pend.append(cp)

    def sib_wait(s, e, h):
        sg = 1 if e == 0 else -1
        slot = og_all.at[zslot(-sg * s, 1 - c, h)]
        copy(slot, slot, s_send.at[e, s, h], s_recv.at[e, s, h], sibling).wait_recv()

    def z_step(s):
        z_ring.step(s, sib_start)

    z_ring.open()
    for h in (0, 1):
        sib_start(0, 0, h)

    for cp in fetch[1:5]:
        cp.wait()
    r_out = lax.broadcasted_iota(jnp.int32, (64, 192), 0)
    r_in = lax.broadcasted_iota(jnp.int32, (64, 192), 1)
    q = lax.rem(r_out, 16)
    pick = (
        (lax.div(r_out, 16) == lax.div(r_in, 48))
        & (lax.div(q, 4) == lax.div(lax.rem(r_in, 48), 16))
        & (q < 12)
        & (lax.rem(y, 4) * 4 + lax.rem(q, 4) == lax.rem(r_in, 16))
    )
    pick = jnp.where(pick, 1.0, 0.0).astype(BF)
    row16 = lax.broadcasted_iota(jnp.int32, (16, B), 0)

    def make_msg(m, carry):
        rows = slab[pl.ds(m * 12, 12)].reshape(192, B)
        picked = jnp.dot(pick, rows, preferred_element_type=F32)
        for u in range(4):
            o = m * 4 + u
            tile = picked[16 * u : 16 * u + 16]
            for s in range(3):
                key = (hb[0, o * 3 + s] - o * ROWS) * 48 + hb[1, o * 3 + s]
                key = jnp.where(s < live[o], key, -1).astype(F32)
                tile = jnp.where(row16 == 12 + s, key, tile)
            msg[o] = tile.astype(BF)
        return carry

    lax.fori_loop(0, NT // 4, make_msg, 0)
    recv[t] = msg[t]

    def a_copy(s):
        o = lax.rem(t + s, NT)
        return copy(msg.at[o], recv.at[t], a_send.at[s], a_recv.at[t], {"tensor": o})

    def a_start(s, carry):
        a_copy(lax.rem(s + NZ - 1, NT)).start()
        return carry

    lax.fori_loop(1, NT // 2 + 1, a_start, 0)
    lax.fori_loop(NT // 2 + 2, NT + 1, a_start, 0)

    z_step(2)

    for cp in fetch[5:]:
        cp.wait()
    o_row = lax.broadcasted_iota(jnp.int32, (B, B), 0)
    o_col = lax.broadcasted_iota(jnp.int32, (B, B), 1)
    to_y = (
        (lax.div(o_row, 16) == lax.rem(lax.div(o_col, 4), NY))
        & (lax.rem(lax.div(o_row, 4), NX) == lax.div(o_col, 32))
        & (lax.rem(o_row, 4) == lax.rem(o_col, 4))
    )
    to_y = jnp.where(to_y, 1.0, 0.0).astype(BF)
    for i in range(ROWS):
        g = gate[:, i * B : (i + 1) * B].astype(F32)
        u = up[:, i * B : (i + 1) * B].astype(F32)
        sig = 1.0 / (1.0 + jnp.exp(-g))
        a = g * sig
        act[:, i * B : (i + 1) * B] = a
        slope_up[:, i * B : (i + 1) * B] = u * (sig * (1.0 + g * (1.0 - sig)))
        hid = (a * u).T.astype(BF)
        hid_t[0, i] = hid
        hid_t[1, i] = jnp.dot(to_y, hid, preferred_element_type=F32).astype(BF)

    lane = lax.broadcasted_iota(jnp.int32, (8, 2 * B), 1)
    block_of = lax.div(lane, 4)
    keycol = jnp.full((8, 2 * B), -100.0, F32)
    for n in range(ROWS * KEEP):
        i, k = (n // 8, n % 8) if n < 40 else ((n - 40) // 4, 8 + n % 4)
        v = (i * 48 + rc[i, k]) * 4
        keycol = jnp.where(block_of == n, v.astype(F32), keycol)
    keycol = (keycol + lax.rem(lane, 4).astype(F32))[0:1]


    def a_wait(s, carry):
        h = lax.rem(t + s, NT)
        copy(msg.at[h], recv.at[h], a_send.at[s], a_recv.at[h], {"tensor": h}).wait_recv()
        return carry

    lax.fori_loop(1, NT, a_wait, 0)

    got = recv[...]
    gotf = got.astype(F32)
    rr = lax.broadcasted_iota(jnp.int32, (NT, 16, B), 1)
    keyrow = jnp.where(
        rr < 4, gotf[:, 12:13, :], jnp.where(rr < 8, gotf[:, 13:14, :], jnp.where(rr < 12, gotf[:, 14:15, :], -1000.0))
    )
    keyrow = (keyrow * 4.0 + lax.rem(rr, 4).astype(F32)).reshape(NT * 16, B)
    got = got.reshape(NT * 16, B)
    for v in range(2):
        hot = jnp.where(keyrow == keycol[:, v * B : (v + 1) * B], 1.0, 0.0).astype(BF)
        res = lax.dot_general(hot, got, (((0,), (0,)), ((), ())), preferred_element_type=F32).astype(BF)
        if v == 0:
            comm_y[y, 0:8] = res.reshape(8, 16, B)
        else:
            comm_y[y, 8:10] = res[:32].reshape(2, 16, B)
            comm_x[x] = res[32:112].reshape(5, 16, B)

    y_ring = Ring(
        RY,
        lambda k, h: comm_y.at[lax.rem(y + k + NY, NY), pl.ds(5 * h, 5)],
        ydev, gy_send, gy_recv,
    )
    wy_ring = Ring(RY, lambda k, h: w_b.at[lax.rem(y + k + NY, NY), h], ydev, wy_send, wy_recv)

    def c_copy(k, back):
        slot = comm_x.at[lax.rem(x - back + NX, NX)]
        return copy(slot, slot, c_send.at[k - 1], c_recv.at[k - 1], xdev(k))

    for k in (2, 1, 3):
        cp = c_copy(k, 0)
        cp.start()
        pend.append(cp)
    y_ring.open()

    z_step(4)
    for k in (1, 3, 2):
        c_copy(k, k).wait_recv()
    s_row = lax.broadcasted_iota(jnp.int32, (64, 64), 0)
    s_col = lax.broadcasted_iota(jnp.int32, (64, 64), 1)
    swap_x = (
        (lax.div(s_row, 16) == lax.rem(lax.div(s_col, 4), 4))
        & (lax.rem(lax.div(s_row, 4), NX) == lax.div(s_col, 16))
        & (lax.rem(s_row, 4) == lax.rem(s_col, 4))
    )
    swap_x = jnp.where(swap_x, 1.0, 0.0).astype(BF)
    for i in range(ROWS):
        res = jnp.dot(swap_x, comm_x[:, i].reshape(64, B), preferred_element_type=F32).astype(BF)
        for u in range(4):
            w_b[y, u // 2, i, :, (u % 2) * B : (u % 2 + 1) * B] = res[16 * u : 16 * u + 16]
    wy_ring.open()
    y_ring.step(2)
    z_step(1)
    z_step(3)
    z_step(6)
    z_step(5)
    for h in (0, 1):
        sib_wait(0, 0, h)
    for s in range(1, RZ + 1):
        for e, h in z_ring.chunks(s):
            sib_wait(s, e, h)

    def products(half):
        def one(i, carry):
            for p in range(2):
                k = half * HALF + 3 * p
                three = jnp.concatenate([og_all[rc[i, k + m]] for m in range(3)], axis=1)
                res = jnp.dot(hid_t[half, i], three, preferred_element_type=F32).astype(BF)
                if half == 0:
                    part_a[:, p, i] = res.reshape(NX, 32, TRI)
                else:
                    part_b[:, p, i] = res.reshape(NY, 16, TRI)
            return carry

        lax.fori_loop(0, ROWS, one, 0)

    def xi(k):
        return lax.rem(x + k + NX, NX)

    def yi(k):
        return lax.rem(y + k + NY, NY)

    def rx(e, j, src, dst):
        return copy(src, dst, rx_send.at[e, j], rx_recv.at[e, j], xdev(1 if e == 0 else -1))

    def begin(cp):
        cp.start()
        pend.append(cp)

    def far(e):
        sg = 1 if e == 0 else -1
        return copy(part_b.at[yi(4), e], far_y.at[e], far_send.at[e], far_recv.at[e], ydev(2 * sg))

    def near(e, p):
        sg = 1 if e == 0 else -1
        return copy(part_b.at[yi(3 * sg), p], near_y.at[e, p], near_send.at[e, p], near_recv.at[e, p], ydev(sg))

    def one_hop(e, p):
        sg = 1 if e == 0 else -1
        return copy(part_b.at[yi(sg), p], one_y.at[e, p], one_send.at[e, p], one_recv.at[e, p], ydev(sg))

    def two_hops(e, p):
        sg = 1 if e == 0 else -1
        return copy(snd_two.at[e, p], two_y.at[e, p], two_send.at[e, p], two_recv.at[e, p], ydev(2 * sg))

    products(1)
    for e in (0, 1):
        begin(far(e))
    for p in (0, 1):
        for e in (0, 1):
            begin(near(e, e if p == 0 else 1 - e))
    products(0)
    begin(rx(0, 0, part_a.at[xi(2), 0], buf_x.at[0]))
    begin(rx(1, 0, part_a.at[xi(2), 1], buf_x.at[1]))
    begin(rx(0, 1, part_a.at[xi(1), 1], fin_x.at[0, 1]))
    begin(rx(1, 1, part_a.at[xi(-1), 0], fin_x.at[1, 0]))
    for p in (0, 1):
        for e in (0, 1):
            begin(one_hop(e, p))

    wy_ring.step(2)
    y_ring.step(1)
    y_ring.step(3)
    y_ring.step(4)
    swap = (
        (lax.div(o_row, 32) == lax.rem(lax.div(o_col, 4), 4))
        & (lax.rem(lax.div(o_row, 4), NY) == lax.div(o_col, 16))
        & (lax.rem(o_row, 4) == lax.rem(o_col, 4))
    )
    swap = jnp.where(swap, 1.0, 0.0).astype(BF)
    for g in range(10):
        res = jnp.dot(swap, comm_y[:, g].reshape(B, B), preferred_element_type=F32).astype(BF)
        for u in range(4):
            n = 4 * g + u
            i, k = n // 8, n % 8
            w_all[x, k // 2, i, :, (k % 2) * B : (k % 2 + 1) * B] = res[32 * u : 32 * u + 32]

    def gx(s, e, q, back):
        sg = 1 if e == 0 else -1
        slot = w_all.at[xi(-sg * back), q]
        return copy(slot, slot, gx_send.at[e, s - 1, q], gx_recv.at[e, s - 1, q], xdev(sg))

    x_all = [(0, 0), (1, 2), (0, 1), (1, 3), (0, 2), (1, 0), (0, 3), (1, 1)]
    for e, q in x_all:
        begin(gx(1, e, q, 0))

    for p in (0, 1):
        for e in (0, 1):
            q = 1 - e if p == 0 else e
            near(e, q).wait_recv()
            sg = 1 if e == 0 else -1
            v = part_b[yi(2 * sg), q].astype(F32) + near_y[e, q].astype(F32)
            if q == e:
                far(e).wait_recv()
                v = v + far_y[e].astype(F32)
            snd_two[e, q] = v.astype(BF)
            begin(two_hops(e, q))
    for e in (0, 1):
        rx(e, 0, part_a.at[xi(2), e], buf_x.at[e]).wait_recv()
        v = part_a[xi(1 if e == 0 else -1), e].astype(F32) + buf_x[e].astype(F32)
        snd_x[e] = v.astype(BF)
        begin(rx(e, 2, snd_x.at[e], fin_x.at[e, e]))

    for e, q in x_all:
        gx(1, e, q, 1).wait_recv()
        if (e, q) in x_all[:4]:
            begin(gx(2, e, q, 1))

    def scatter(own, groups, dst, i):
        low = lax.broadcasted_iota(jnp.int32, (groups, 8, B), 1) < 4
        own = own.reshape(groups, 8, HALF * B)
        for p in range(HALF // 2):
            a0 = own[:, :, 2 * p * B : (2 * p + 1) * B]
            a1 = own[:, :, (2 * p + 1) * B : (2 * p + 2) * B]
            first = (i * HALF + 2 * p) * 4
            dst[:, 0, first : first + 8, :] = jnp.where(low, a0, pltpu.roll(a1, 4, 1))
            dst[:, 1, first : first + 8, :] = jnp.where(low, pltpu.roll(a0, 4, 1), a1)

    for e in (0, 1):
        rx(e, 1, part_a.at[xi(1), 1 - e], fin_x.at[e, 1 - e]).wait_recv()
        rx(e, 2, snd_x.at[e], fin_x.at[e, e]).wait_recv()
    yin[:, :, HROW:, :] = jnp.zeros((NY // 2, 2, B - HROW, B), F32)
    for i in range(ROWS):
        own = [
            part_a[x, p, i].astype(F32) + fin_x[0, p, i].astype(F32) + fin_x[1, p, i].astype(F32) for p in (0, 1)
        ]
        scatter(jnp.concatenate(own, axis=1), NY // 2, yin, i)
    snd_ya[...] = yin[...].reshape(NY, B, B).astype(BF)

    def ya(k):
        return copy(snd_ya.at[yi(k)], rcv_ya.at[k - 1], ya_send.at[k - 1], ya_recv.at[k - 1], ydev(k))

    for k in (4, 3, 5, 2, 6, 1, 7):
        begin(ya(k))

    for e in (0, 1):
        for p in (0, 1):
            one_hop(e, p).wait_recv()
            two_hops(e, p).wait_recv()
    xin[:, :, HROW:, :] = jnp.zeros((NX // 2, 2, B - HROW, B), F32)
    for i in range(ROWS):
        own = [
            part_b[y, p, i].astype(F32) + one_y[0, p, i].astype(F32) + one_y[1, p, i].astype(F32)
            + two_y[0, p, i].astype(F32) + two_y[1, p, i].astype(F32)
            for p in (0, 1)
        ]
        scatter(jnp.concatenate(own, axis=1), NX // 2, xin, i)
    snd_xb[...] = xin[...].reshape(NX, B, B).astype(BF)

    def xb(k):
        return copy(snd_xb.at[xi(k)], rcv_xb.at[k - 1], xb_send.at[k - 1], xb_recv.at[k - 1], xdev(k))

    for k in (2, 1, 3):
        begin(xb(k))

    for e, q in x_all[:4]:
        gx(2, e, q, 2).wait_recv()

    wy_ring.step(1)
    wy_ring.step(3)
    wy_ring.step(4)

    def hidden_grad(i, carry):
        total = jnp.zeros((B, B), F32)
        for q in range(6):
            left = jnp.concatenate([og_all[rc[i, q * 2 + m]] for m in range(2)], axis=1)
            if q < 4:
                right = w_all[:, q, i].reshape(B, 2 * B)
            else:
                right = w_b[:, q - 4, i].reshape(B, 2 * B)
                right = jnp.dot(swap, right, preferred_element_type=F32).astype(BF)
            total = total + lax.dot_general(left, right, (((1,), (1,)), ((), ())), preferred_element_type=F32)
        cols = pl.ds(pl.multiple_of(i * B, B), B)
        gg[:, cols] = (total * slope_up[:, cols]).astype(BF)
        ug[:, cols] = (total * act[:, cols]).astype(BF)
        return carry

    lax.fori_loop(0, ROWS, hidden_grad, 0)
    gg_out = pltpu.make_async_copy(gg, gg_hbm, out_sem.at[0])
    gg_out.start()
    ug_out = pltpu.make_async_copy(ug, ug_hbm, out_sem.at[1])
    ug_out.start()

    for half, n, mine, box, cps in (
        (0, NY, yin[lax.div(y, 2), lax.rem(y, 2)], rcv_ya, ya),
        (1, NX, xin[lax.div(x, 2), lax.rem(x, 2)], rcv_xb, xb),
    ):
        for k in range(1, n):
            cps(k).wait_recv()
            mine = mine + box[k - 1].astype(F32)
        for i in range(ROWS):
            first = (i * KEEP + half * HALF) * 4
            wgf[first : first + 4 * HALF, :] = mine[i * 4 * HALF : (i + 1) * 4 * HALF]
    for a in range(4):
        wg[:, a * B : (a + 1) * B] = wgf[pl.ds(a, ROWS * KEEP, stride=4), :].astype(BF)
    wg_out = pltpu.make_async_copy(wg, wg_hbm, out_sem.at[2])
    wg_out.start()

    def a_done(s, carry):
        a_copy(s).wait_send()
        return carry

    lax.fori_loop(1, NT, a_done, 0)
    for cp in pend:
        cp.wait_send()
    for cp in (gg_out, ug_out, wg_out):
        cp.wait()


def local(gate_pre, up_pre, out_grad, weight_slots, holder_blocks, holder_live_slots, row_columns):
    hbm = pl.BlockSpec(memory_space=pl.ANY)
    dma = pltpu.SemaphoreType.DMA
    gate_grad, up_grad, weight_grad = pl.pallas_call(
        kernel,
        out_shape=(
            jax.ShapeDtypeStruct(gate_pre.shape, BF),
            jax.ShapeDtypeStruct(gate_pre.shape, BF),
            jax.ShapeDtypeStruct((ROWS * KEEP, 4 * B), BF),
        ),
        in_specs=[hbm] * 7,
        out_specs=(hbm, hbm, hbm),
        scratch_shapes=[
            pltpu.VMEM(gate_pre.shape, BF), pltpu.VMEM(up_pre.shape, BF), pltpu.VMEM(out_grad.shape, BF),
            pltpu.SMEM((2, 3 * NT), jnp.int32), pltpu.SMEM((NT,), jnp.int32), pltpu.SMEM((ROWS, KEEP), jnp.int32),
            pltpu.VMEM(gate_pre.shape, BF), pltpu.VMEM(gate_pre.shape, BF), pltpu.VMEM((ROWS * KEEP, 4 * B), BF),
            pltpu.VMEM((2 * NT, B, B), BF),
            pltpu.VMEM((3 * NT, 16, B), BF),
            pltpu.VMEM((NT, 16, B), BF),
            pltpu.VMEM((NT, 16, B), BF),
            pltpu.VMEM((NY, 10, 16, B), BF),
            pltpu.VMEM((NX, 5, 16, B), BF),
            pltpu.VMEM((NX, 4, ROWS, 32, 2 * B), BF),
            pltpu.VMEM((NY, 2, ROWS, 16, 2 * B), BF),
            pltpu.VMEM((B, ROWS * B), F32),
            pltpu.VMEM((B, ROWS * B), F32),
            pltpu.VMEM((2, ROWS, B, B), BF),
            pltpu.VMEM((NX, 2, ROWS, 32, TRI), BF),
            pltpu.VMEM((NY, 2, ROWS, 16, TRI), BF),
            pltpu.VMEM((2, ROWS, 32, TRI), BF),
            pltpu.VMEM((2, 2, ROWS, 32, TRI), BF),
            pltpu.VMEM((2, ROWS, 32, TRI), BF),
            pltpu.VMEM((2, ROWS, 16, TRI), BF),
            pltpu.VMEM((2, 2, ROWS, 16, TRI), BF),
            pltpu.VMEM((2, 2, ROWS, 16, TRI), BF),
            pltpu.VMEM((2, 2, ROWS, 16, TRI), BF),
            pltpu.VMEM((2, 2, ROWS, 16, TRI), BF),
            pltpu.VMEM((NY // 2, 2, B, B), F32),
            pltpu.VMEM((NY, B, B), BF), pltpu.VMEM((NY - 1, B, B), BF),
            pltpu.VMEM((NX // 2, 2, B, B), F32),
            pltpu.VMEM((NX, B, B), BF), pltpu.VMEM((NX - 1, B, B), BF),
            pltpu.VMEM((NROW, B), F32),
            dma((7,)), dma((3,)),
            dma((2, RZ, 2)), dma((2, RZ, 2)),
            dma((2, RZ + 1, 2)), dma((2, RZ + 1, 2)),
            dma((NT,)), dma((NT,)),
            dma((2, RY, 2)), dma((2, RY, 2)),
            dma((2, 2, 4)), dma((2, 2, 4)),
            dma((NX - 1,)), dma((NX - 1,)), dma((2, RY, 2)), dma((2, RY, 2)),
            dma((2, 3)), dma((2, 3)),
            dma((2,)), dma((2,)), dma((2, 2)), dma((2, 2)),
            dma((2, 2)), dma((2, 2)), dma((2, 2)), dma((2, 2)),
            dma((NY - 1,)), dma((NY - 1,)), dma((NX - 1,)), dma((NX - 1,)),
        ],
        compiler_params=pltpu.CompilerParams(
            collective_id=0, has_side_effects=True, vmem_limit_bytes=62 * 1024 * 1024
        ),
        cost_estimate=pl.CostEstimate(flops=600_000_000, bytes_accessed=4_000_000, transcendentals=82_000),
    )(gate_pre, up_pre, out_grad, weight_slots, holder_blocks.T, holder_live_slots, row_columns)
    return gate_grad, up_grad, weight_grad


def solution(mesh):
    placed = (
        P("dp", "tensor"),
        P("dp", "tensor"),
        P("dp", "tensor"),
        P("tensor", None, None),
        P("tensor", None),
        P("tensor"),
        P("tensor", None),
    )
    return jax.shard_map(
        local,
        mesh=mesh,
        in_specs=placed,
        out_specs=(P("dp", "tensor"), P("dp", "tensor"), P("tensor", "dp")),
        check_vma=False,
    )
```

```python
import jax
import jax.numpy as jnp
from jax import lax
from jax.experimental import pallas as pl
from jax.experimental.pallas import tpu as pltpu
from jax.sharding import PartitionSpec as P

MESH = pl.DeviceIdType.MESH
NX, NY, NZ = 4, 8, 12
NT = 2 * NZ
RZ, RY = NZ // 2, NY // 2
ROWS, KEEP, B = 5, 12, 128
HALF = KEEP // 2
TRI = 3 * B
BF, F32 = jnp.bfloat16, jnp.float32
NROW = ROWS * KEEP * 4
HROW = NROW // 2


def kernel(
    gate_hbm, up_hbm, og_hbm, w_hbm, hb_hbm, live_hbm, rc_hbm,
    hg_hbm, wg_hbm,
    gate, up, og, hb, live, rc, hg, wg,
    og_all, slab, msg, recv, comm_y, comm_x, w_all, w_b, hid_t, part_a, part_b,
    buf_x, fin_x, snd_x, far_y, near_y, one_y, two_y, snd_two, yin, snd_ya, rcv_ya, xin, snd_xb, rcv_xb, wgf,
    in_sem, out_sem, z_send, z_recv, s_send, s_recv, a_send, a_recv, gy_send, gy_recv, gx_send, gx_recv, c_send, c_recv, wy_send, wy_recv,
    rx_send, rx_recv, far_send, far_recv, near_send, near_recv, one_send, one_recv, two_send, two_recv,
    ya_send, ya_recv, xb_send, xb_recv,
):
    t, d = lax.axis_index("tensor"), lax.axis_index("dp")
    z, c = lax.div(t, 2), lax.rem(t, 2)
    x, y = lax.div(d, NY), lax.rem(d, NY)

    def zdev(k):
        return {"tensor": lax.rem(z + k + NZ, NZ) * 2 + c}

    def xdev(k):
        return {"dp": lax.rem(x + k + NX, NX) * NY + y}

    def ydev(k):
        return {"dp": x * NY + lax.rem(y + k + NY, NY)}

    sibling = {"tensor": z * 2 + (1 - c)}

    def copy(src, dst, ss, rs, dev):
        return pltpu.make_async_remote_copy(
            src_ref=src, dst_ref=dst, send_sem=ss, recv_sem=rs, device_id=dev, device_id_type=MESH
        )

    fetch = [
        pltpu.make_async_copy(src, dst, in_sem.at[n])
        for n, (src, dst) in enumerate([
            (og_hbm, og), (w_hbm.at[:, pl.ds(pl.multiple_of(x * 32 + lax.div(y, 4) * 16, 16), 16), :], slab), (hb_hbm, hb),
            (live_hbm, live), (rc_hbm, rc), (gate_hbm, gate), (up_hbm, up),
        ])
    ]
    for cp in fetch:
        cp.start()

    barrier = pltpu.get_barrier_semaphore()

    def greet(s, carry):
        pl.semaphore_signal(barrier, inc=1, device_id={"tensor": lax.rem(t + s, NT)}, device_id_type=MESH)
        return carry

    lax.fori_loop(1, NT, greet, 0)
    for k in (1, 2, 3):
        pl.semaphore_signal(barrier, inc=1, device_id=xdev(k), device_id_type=MESH)
    for k in range(1, NY):
        pl.semaphore_signal(barrier, inc=1, device_id=ydev(k), device_id_type=MESH)
    pend = []

    fetch[0].wait()
    og_all[2 * t] = og[:, :B]
    og_all[2 * t + 1] = og[:, B:]
    pl.semaphore_wait(barrier, NT - 1 + NX - 1 + NY - 1)

    def zslot(k, cc, h):
        return 2 * (lax.rem(z + k + NZ, NZ) * 2 + cc) + h

    class Ring:
        def __init__(self, radius, slot, dev, send, recv):
            self.radius, self.slot, self.dev, self.send, self.recv = radius, slot, dev, send, recv

        def chunks(self, s):
            return [(0, 0), (1, 1), (0, 1), (1, 0)][: 4 if s < self.radius else 2 if s == self.radius else 0]

        def copy(self, s, k, e, h):
            sg = 1 if e == 0 else -1
            slot = self.slot(-sg * s, h)
            return copy(slot, slot, self.send.at[e, s + k - 1, h], self.recv.at[e, s + k - 1, h], self.dev(sg * k))

        def start(self, s, e, h, ks=(2, 1)):
            for k in ks:
                if (e, h) in self.chunks(s + k):
                    cp = self.copy(s, k, e, h)
                    cp.start()
                    pend.append(cp)

        def open(self):
            for k in (2, 1):
                for e, h in self.chunks(1):
                    self.start(0, e, h, (k,))

        def step(self, s, arrived=None):
            for e, h in self.chunks(s):
                sg = 1 if e == 0 else -1
                slot = self.slot(-sg * s, h)
                copy(slot, slot, self.send.at[e, s - 1, h], self.recv.at[e, s - 1, h], self.dev(sg)).wait_recv()
                if s % 2 == 0:
                    self.start(s, e, h)
                if arrived is not None:
                    arrived(s, e, h)

    z_ring = Ring(RZ, lambda k, h: og_all.at[zslot(k, c, h)], zdev, z_send, z_recv)

    def sib_start(s, e, h):
        sg = 1 if e == 0 else -1
        slot = og_all.at[zslot(-sg * s, c, h)]
        cp = copy(slot, slot, s_send.at[e, s, h], s_recv.at[e, s, h], sibling)
        cp.start()
        pend.append(cp)

    def sib_wait(s, e, h):
        sg = 1 if e == 0 else -1
        slot = og_all.at[zslot(-sg * s, 1 - c, h)]
        copy(slot, slot, s_send.at[e, s, h], s_recv.at[e, s, h], sibling).wait_recv()

    def z_step(s):
        z_ring.step(s, sib_start)

    z_ring.open()
    for h in (0, 1):
        sib_start(0, 0, h)

    for cp in fetch[1:5]:
        cp.wait()
    r_out = lax.broadcasted_iota(jnp.int32, (64, 192), 0)
    r_in = lax.broadcasted_iota(jnp.int32, (64, 192), 1)
    q = lax.rem(r_out, 16)
    pick = (
        (lax.div(r_out, 16) == lax.div(r_in, 48))
        & (lax.div(q, 4) == lax.div(lax.rem(r_in, 48), 16))
        & (q < 12)
        & (lax.rem(y, 4) * 4 + lax.rem(q, 4) == lax.rem(r_in, 16))
    )
    pick = jnp.where(pick, 1.0, 0.0).astype(BF)
    row16 = lax.broadcasted_iota(jnp.int32, (16, B), 0)

    def make_msg(m, carry):
        rows = slab[pl.ds(m * 12, 12)].reshape(192, B)
        picked = jnp.dot(pick, rows, preferred_element_type=F32)
        for u in range(4):
            o = m * 4 + u
            tile = picked[16 * u : 16 * u + 16]
            for s in range(3):
                key = (hb[0, o * 3 + s] - o * ROWS) * 48 + hb[1, o * 3 + s]
                key = jnp.where(s < live[o], key, -1).astype(F32)
                tile = jnp.where(row16 == 12 + s, key, tile)
            msg[o] = tile.astype(BF)
        return carry

    lax.fori_loop(0, NT // 4, make_msg, 0)
    recv[t] = msg[t]

    def a_copy(s):
        o = lax.rem(t + s, NT)
        return copy(msg.at[o], recv.at[t], a_send.at[s], a_recv.at[t], {"tensor": o})

    def a_start(s, carry):
        a_copy(lax.rem(s + NZ - 1, NT)).start()
        return carry

    lax.fori_loop(1, NT // 2 + 1, a_start, 0)
    lax.fori_loop(NT // 2 + 2, NT + 1, a_start, 0)

    z_step(2)

    for cp in fetch[5:]:
        cp.wait()
    o_row = lax.broadcasted_iota(jnp.int32, (B, B), 0)
    o_col = lax.broadcasted_iota(jnp.int32, (B, B), 1)
    to_y = (
        (lax.div(o_row, 16) == lax.rem(lax.div(o_col, 4), NY))
        & (lax.rem(lax.div(o_row, 4), NX) == lax.div(o_col, 32))
        & (lax.rem(o_row, 4) == lax.rem(o_col, 4))
    )
    to_y = jnp.where(to_y, 1.0, 0.0).astype(BF)
    for i in range(ROWS):
        g = gate[:, i * B : (i + 1) * B].astype(F32)
        u = up[:, i * B : (i + 1) * B].astype(F32)
        sig = 1.0 / (1.0 + jnp.exp(-g))
        a = g * sig
        hid = (a * u).T.astype(BF)
        hid_t[0, i] = hid
        hid_t[1, i] = jnp.dot(to_y, hid, preferred_element_type=F32).astype(BF)

    lane = lax.broadcasted_iota(jnp.int32, (8, 2 * B), 1)
    block_of = lax.div(lane, 4)
    keycol = jnp.full((8, 2 * B), -100.0, F32)
    for n in range(ROWS * KEEP):
        i, k = (n // 8, n % 8) if n < 40 else ((n - 40) // 4, 8 + n % 4)
        v = (i * 48 + rc[i, k]) * 4
        keycol = jnp.where(block_of == n, v.astype(F32), keycol)
    keycol = (keycol + lax.rem(lane, 4).astype(F32))[0:1]


    def a_wait(s, carry):
        h = lax.rem(t + s, NT)
        copy(msg.at[h], recv.at[h], a_send.at[s], a_recv.at[h], {"tensor": h}).wait_recv()
        return carry

    lax.fori_loop(1, NT, a_wait, 0)

    got = recv[...]
    gotf = got.astype(F32)
    rr = lax.broadcasted_iota(jnp.int32, (NT, 16, B), 1)
    keyrow = jnp.where(
        rr < 4, gotf[:, 12:13, :], jnp.where(rr < 8, gotf[:, 13:14, :], jnp.where(rr < 12, gotf[:, 14:15, :], -1000.0))
    )
    keyrow = (keyrow * 4.0 + lax.rem(rr, 4).astype(F32)).reshape(NT * 16, B)
    got = got.reshape(NT * 16, B)
    for v in range(2):
        hot = jnp.where(keyrow == keycol[:, v * B : (v + 1) * B], 1.0, 0.0).astype(BF)
        res = lax.dot_general(hot, got, (((0,), (0,)), ((), ())), preferred_element_type=F32).astype(BF)
        if v == 0:
            comm_y[y, 0:8] = res.reshape(8, 16, B)
        else:
            comm_y[y, 8:10] = res[:32].reshape(2, 16, B)
            comm_x[x] = res[32:112].reshape(5, 16, B)

    y_ring = Ring(
        RY,
        lambda k, h: comm_y.at[lax.rem(y + k + NY, NY), pl.ds(5 * h, 5)],
        ydev, gy_send, gy_recv,
    )
    wy_ring = Ring(RY, lambda k, h: w_b.at[lax.rem(y + k + NY, NY), h], ydev, wy_send, wy_recv)

    def c_copy(k, back):
        slot = comm_x.at[lax.rem(x - back + NX, NX)]
        return copy(slot, slot, c_send.at[k - 1], c_recv.at[k - 1], xdev(k))

    for k in (2, 1, 3):
        cp = c_copy(k, 0)
        cp.start()
        pend.append(cp)
    y_ring.open()

    z_step(4)
    for k in (1, 3, 2):
        c_copy(k, k).wait_recv()
    s_row = lax.broadcasted_iota(jnp.int32, (64, 64), 0)
    s_col = lax.broadcasted_iota(jnp.int32, (64, 64), 1)
    swap_x = (
        (lax.div(s_row, 16) == lax.rem(lax.div(s_col, 4), 4))
        & (lax.rem(lax.div(s_row, 4), NX) == lax.div(s_col, 16))
        & (lax.rem(s_row, 4) == lax.rem(s_col, 4))
    )
    swap_x = jnp.where(swap_x, 1.0, 0.0).astype(BF)
    for i in range(ROWS):
        res = jnp.dot(swap_x, comm_x[:, i].reshape(64, B), preferred_element_type=F32).astype(BF)
        for u in range(4):
            w_b[y, u // 2, i, :, (u % 2) * B : (u % 2 + 1) * B] = res[16 * u : 16 * u + 16]
    wy_ring.open()
    y_ring.step(2)
    z_step(1)
    z_step(3)
    z_step(6)
    z_step(5)
    for h in (0, 1):
        sib_wait(0, 0, h)
    for s in range(1, RZ + 1):
        for e, h in z_ring.chunks(s):
            sib_wait(s, e, h)

    def products(half):
        def one(i, carry):
            for p in range(2):
                k = half * HALF + 3 * p
                three = jnp.concatenate([og_all[rc[i, k + m]] for m in range(3)], axis=1)
                res = jnp.dot(hid_t[half, i], three, preferred_element_type=F32).astype(BF)
                if half == 0:
                    part_a[:, p, i] = res.reshape(NX, 32, TRI)
                else:
                    part_b[:, p, i] = res.reshape(NY, 16, TRI)
            return carry

        lax.fori_loop(0, ROWS, one, 0)

    def xi(k):
        return lax.rem(x + k + NX, NX)

    def yi(k):
        return lax.rem(y + k + NY, NY)

    def rx(e, j, src, dst):
        return copy(src, dst, rx_send.at[e, j], rx_recv.at[e, j], xdev(1 if e == 0 else -1))

    def begin(cp):
        cp.start()
        pend.append(cp)

    def far(e):
        sg = 1 if e == 0 else -1
        return copy(part_b.at[yi(4), e], far_y.at[e], far_send.at[e], far_recv.at[e], ydev(2 * sg))

    def near(e, p):
        sg = 1 if e == 0 else -1
        return copy(part_b.at[yi(3 * sg), p], near_y.at[e, p], near_send.at[e, p], near_recv.at[e, p], ydev(sg))

    def one_hop(e, p):
        sg = 1 if e == 0 else -1
        return copy(part_b.at[yi(sg), p], one_y.at[e, p], one_send.at[e, p], one_recv.at[e, p], ydev(sg))

    def two_hops(e, p):
        sg = 1 if e == 0 else -1
        return copy(snd_two.at[e, p], two_y.at[e, p], two_send.at[e, p], two_recv.at[e, p], ydev(2 * sg))

    products(1)
    for e in (0, 1):
        begin(far(e))
    for p in (0, 1):
        for e in (0, 1):
            begin(near(e, e if p == 0 else 1 - e))
    products(0)
    begin(rx(0, 0, part_a.at[xi(2), 0], buf_x.at[0]))
    begin(rx(1, 0, part_a.at[xi(2), 1], buf_x.at[1]))
    begin(rx(0, 1, part_a.at[xi(1), 1], fin_x.at[0, 1]))
    begin(rx(1, 1, part_a.at[xi(-1), 0], fin_x.at[1, 0]))
    for p in (0, 1):
        for e in (0, 1):
            begin(one_hop(e, p))

    wy_ring.step(2)
    y_ring.step(1)
    y_ring.step(3)
    y_ring.step(4)
    swap = (
        (lax.div(o_row, 32) == lax.rem(lax.div(o_col, 4), 4))
        & (lax.rem(lax.div(o_row, 4), NY) == lax.div(o_col, 16))
        & (lax.rem(o_row, 4) == lax.rem(o_col, 4))
    )
    swap = jnp.where(swap, 1.0, 0.0).astype(BF)
    for g in range(10):
        res = jnp.dot(swap, comm_y[:, g].reshape(B, B), preferred_element_type=F32).astype(BF)
        for u in range(4):
            n = 4 * g + u
            i, k = n // 8, n % 8
            w_all[x, k // 2, i, :, (k % 2) * B : (k % 2 + 1) * B] = res[32 * u : 32 * u + 32]

    def gx(s, e, q, back):
        sg = 1 if e == 0 else -1
        slot = w_all.at[xi(-sg * back), q]
        return copy(slot, slot, gx_send.at[e, s - 1, q], gx_recv.at[e, s - 1, q], xdev(sg))

    x_all = [(0, 0), (1, 2), (0, 1), (1, 3), (0, 2), (1, 0), (0, 3), (1, 1)]
    for e, q in x_all:
        begin(gx(1, e, q, 0))

    for p in (0, 1):
        for e in (0, 1):
            q = 1 - e if p == 0 else e
            near(e, q).wait_recv()
            sg = 1 if e == 0 else -1
            v = part_b[yi(2 * sg), q].astype(F32) + near_y[e, q].astype(F32)
            if q == e:
                far(e).wait_recv()
                v = v + far_y[e].astype(F32)
            snd_two[e, q] = v.astype(BF)
            begin(two_hops(e, q))
    for e in (0, 1):
        rx(e, 0, part_a.at[xi(2), e], buf_x.at[e]).wait_recv()
        v = part_a[xi(1 if e == 0 else -1), e].astype(F32) + buf_x[e].astype(F32)
        snd_x[e] = v.astype(BF)
        begin(rx(e, 2, snd_x.at[e], fin_x.at[e, e]))

    for e, q in x_all:
        gx(1, e, q, 1).wait_recv()
        if (e, q) in x_all[:4]:
            begin(gx(2, e, q, 1))

    def scatter(own, groups, dst, i):
        low = lax.broadcasted_iota(jnp.int32, (groups, 8, B), 1) < 4
        own = own.reshape(groups, 8, HALF * B)
        for p in range(HALF // 2):
            a0 = own[:, :, 2 * p * B : (2 * p + 1) * B]
            a1 = own[:, :, (2 * p + 1) * B : (2 * p + 2) * B]
            first = (i * HALF + 2 * p) * 4
            dst[:, 0, first : first + 8, :] = jnp.where(low, a0, pltpu.roll(a1, 4, 1))
            dst[:, 1, first : first + 8, :] = jnp.where(low, pltpu.roll(a0, 4, 1), a1)

    for e in (0, 1):
        rx(e, 1, part_a.at[xi(1), 1 - e], fin_x.at[e, 1 - e]).wait_recv()
        rx(e, 2, snd_x.at[e], fin_x.at[e, e]).wait_recv()
    yin[:, :, HROW:, :] = jnp.zeros((NY // 2, 2, B - HROW, B), F32)
    for i in range(ROWS):
        own = [
            part_a[x, p, i].astype(F32) + fin_x[0, p, i].astype(F32) + fin_x[1, p, i].astype(F32) for p in (0, 1)
        ]
        scatter(jnp.concatenate(own, axis=1), NY // 2, yin, i)
    snd_ya[...] = yin[...].reshape(NY, B, B).astype(BF)

    def ya(k):
        return copy(snd_ya.at[yi(k)], rcv_ya.at[k - 1], ya_send.at[k - 1], ya_recv.at[k - 1], ydev(k))

    for k in (4, 3, 5, 2, 6, 1, 7):
        begin(ya(k))

    for e in (0, 1):
        for p in (0, 1):
            one_hop(e, p).wait_recv()
            two_hops(e, p).wait_recv()
    xin[:, :, HROW:, :] = jnp.zeros((NX // 2, 2, B - HROW, B), F32)
    for i in range(ROWS):
        own = [
            part_b[y, p, i].astype(F32) + one_y[0, p, i].astype(F32) + one_y[1, p, i].astype(F32)
            + two_y[0, p, i].astype(F32) + two_y[1, p, i].astype(F32)
            for p in (0, 1)
        ]
        scatter(jnp.concatenate(own, axis=1), NX // 2, xin, i)
    snd_xb[...] = xin[...].reshape(NX, B, B).astype(BF)

    def xb(k):
        return copy(snd_xb.at[xi(k)], rcv_xb.at[k - 1], xb_send.at[k - 1], xb_recv.at[k - 1], xdev(k))

    for k in (2, 1, 3):
        begin(xb(k))

    for e, q in x_all[:4]:
        gx(2, e, q, 2).wait_recv()

    wy_ring.step(1)
    wy_ring.step(3)
    wy_ring.step(4)

    def hidden_grad(i, carry):
        total = jnp.zeros((B, B), F32)
        for q in range(6):
            left = jnp.concatenate([og_all[rc[i, q * 2 + m]] for m in range(2)], axis=1)
            if q < 4:
                right = w_all[:, q, i].reshape(B, 2 * B)
            else:
                right = w_b[:, q - 4, i].reshape(B, 2 * B)
                right = jnp.dot(swap, right, preferred_element_type=F32).astype(BF)
            total = total + lax.dot_general(left, right, (((1,), (1,)), ((), ())), preferred_element_type=F32)
        cols = pl.ds(pl.multiple_of(i * B, B), B)
        hg[:, cols] = total
        return carry

    lax.fori_loop(0, ROWS, hidden_grad, 0)
    hg_out = pltpu.make_async_copy(hg, hg_hbm, out_sem.at[0])
    hg_out.start()

    for half, n, mine, box, cps in (
        (0, NY, yin[lax.div(y, 2), lax.rem(y, 2)], rcv_ya, ya),
        (1, NX, xin[lax.div(x, 2), lax.rem(x, 2)], rcv_xb, xb),
    ):
        for k in range(1, n):
            cps(k).wait_recv()
            mine = mine + box[k - 1].astype(F32)
        for i in range(ROWS):
            first = (i * KEEP + half * HALF) * 4
            wgf[first : first + 4 * HALF, :] = mine[i * 4 * HALF : (i + 1) * 4 * HALF]
    for a in range(4):
        wg[:, a * B : (a + 1) * B] = wgf[pl.ds(a, ROWS * KEEP, stride=4), :].astype(BF)
    wg_out = pltpu.make_async_copy(wg, wg_hbm, out_sem.at[1])
    wg_out.start()

    def a_done(s, carry):
        a_copy(s).wait_send()
        return carry

    lax.fori_loop(1, NT, a_done, 0)
    for cp in pend:
        cp.wait_send()
    for cp in (hg_out, wg_out):
        cp.wait()


def local(gate_pre, up_pre, out_grad, weight_slots, holder_blocks, holder_live_slots, row_columns):
    hbm = pl.BlockSpec(memory_space=pl.ANY)
    dma = pltpu.SemaphoreType.DMA
    hidden_grad, weight_grad = pl.pallas_call(
        kernel,
        out_shape=(
            jax.ShapeDtypeStruct(gate_pre.shape, F32),
            jax.ShapeDtypeStruct((ROWS * KEEP, 4 * B), BF),
        ),
        in_specs=[hbm] * 7,
        out_specs=(hbm, hbm),
        scratch_shapes=[
            pltpu.VMEM(gate_pre.shape, BF), pltpu.VMEM(up_pre.shape, BF), pltpu.VMEM(out_grad.shape, BF),
            pltpu.SMEM((2, 3 * NT), jnp.int32), pltpu.SMEM((NT,), jnp.int32), pltpu.SMEM((ROWS, KEEP), jnp.int32),
            pltpu.VMEM(gate_pre.shape, F32), pltpu.VMEM((ROWS * KEEP, 4 * B), BF),
            pltpu.VMEM((2 * NT, B, B), BF),
            pltpu.VMEM((3 * NT, 16, B), BF),
            pltpu.VMEM((NT, 16, B), BF),
            pltpu.VMEM((NT, 16, B), BF),
            pltpu.VMEM((NY, 10, 16, B), BF),
            pltpu.VMEM((NX, 5, 16, B), BF),
            pltpu.VMEM((NX, 4, ROWS, 32, 2 * B), BF),
            pltpu.VMEM((NY, 2, ROWS, 16, 2 * B), BF),
            pltpu.VMEM((2, ROWS, B, B), BF),
            pltpu.VMEM((NX, 2, ROWS, 32, TRI), BF),
            pltpu.VMEM((NY, 2, ROWS, 16, TRI), BF),
            pltpu.VMEM((2, ROWS, 32, TRI), BF),
            pltpu.VMEM((2, 2, ROWS, 32, TRI), BF),
            pltpu.VMEM((2, ROWS, 32, TRI), BF),
            pltpu.VMEM((2, ROWS, 16, TRI), BF),
            pltpu.VMEM((2, 2, ROWS, 16, TRI), BF),
            pltpu.VMEM((2, 2, ROWS, 16, TRI), BF),
            pltpu.VMEM((2, 2, ROWS, 16, TRI), BF),
            pltpu.VMEM((2, 2, ROWS, 16, TRI), BF),
            pltpu.VMEM((NY // 2, 2, B, B), F32),
            pltpu.VMEM((NY, B, B), BF), pltpu.VMEM((NY - 1, B, B), BF),
            pltpu.VMEM((NX // 2, 2, B, B), F32),
            pltpu.VMEM((NX, B, B), BF), pltpu.VMEM((NX - 1, B, B), BF),
            pltpu.VMEM((NROW, B), F32),
            dma((7,)), dma((2,)),
            dma((2, RZ, 2)), dma((2, RZ, 2)),
            dma((2, RZ + 1, 2)), dma((2, RZ + 1, 2)),
            dma((NT,)), dma((NT,)),
            dma((2, RY, 2)), dma((2, RY, 2)),
            dma((2, 2, 4)), dma((2, 2, 4)),
            dma((NX - 1,)), dma((NX - 1,)), dma((2, RY, 2)), dma((2, RY, 2)),
            dma((2, 3)), dma((2, 3)),
            dma((2,)), dma((2,)), dma((2, 2)), dma((2, 2)),
            dma((2, 2)), dma((2, 2)), dma((2, 2)), dma((2, 2)),
            dma((NY - 1,)), dma((NY - 1,)), dma((NX - 1,)), dma((NX - 1,)),
        ],
        compiler_params=pltpu.CompilerParams(
            collective_id=0, has_side_effects=True, vmem_limit_bytes=62 * 1024 * 1024
        ),
        cost_estimate=pl.CostEstimate(flops=600_000_000, bytes_accessed=4_000_000, transcendentals=82_000),
    )(gate_pre, up_pre, out_grad, weight_slots, holder_blocks.T, holder_live_slots, row_columns)
    g, u = gate_pre.astype(F32), up_pre.astype(F32)
    sig = jax.nn.sigmoid(g)
    gate_grad = (hidden_grad * u * (sig * (1.0 + g * (1.0 - sig)))).astype(BF)
    up_grad = (hidden_grad * (g * sig)).astype(BF)
    return gate_grad, up_grad, weight_grad


def solution(mesh):
    placed = (
        P("dp", "tensor"),
        P("dp", "tensor"),
        P("dp", "tensor"),
        P("tensor", None, None),
        P("tensor", None),
        P("tensor"),
        P("tensor", None),
    )
    return jax.shard_map(
        local,
        mesh=mesh,
        in_specs=placed,
        out_specs=(P("dp", "tensor"), P("dp", "tensor"), P("tensor", "dp")),
        check_vma=False,
    )
```

```python
import jax
import jax.numpy as jnp
from jax import lax
from jax.experimental import pallas as pl
from jax.experimental.pallas import tpu as pltpu
from jax.sharding import PartitionSpec as P

MESH = pl.DeviceIdType.MESH
NX, NY, NZ = 4, 8, 12
NT = 2 * NZ
RZ, RY = NZ // 2, NY // 2
ROWS, KEEP, B = 5, 12, 128
HALF = KEEP // 2
TRI = 3 * B
BF, F32 = jnp.bfloat16, jnp.float32
NROW = ROWS * KEEP * 4
HROW = NROW // 2


def kernel(
    gate_hbm, up_hbm, og_hbm, w_hbm, hb_hbm, live_hbm, rc_hbm,
    hg_hbm, wg_hbm,
    gate, up, og, hb, live, rc, hg, wg,
    og_all, slab, msg, recv, comm_y, comm_x, w_all, w_b, hid_t, part_a, part_b,
    buf_x, fin_x, snd_x, far_y, near_y, one_y, two_y, snd_two, yin, snd_ya, rcv_ya, xin, snd_xb, rcv_xb, wgf,
    in_sem, out_sem, z_send, z_recv, s_send, s_recv, a_send, a_recv, gy_send, gy_recv, gx_send, gx_recv, c_send, c_recv, wy_send, wy_recv,
    rx_send, rx_recv, far_send, far_recv, near_send, near_recv, one_send, one_recv, two_send, two_recv,
    ya_send, ya_recv, xb_send, xb_recv,
):
    t, d = lax.axis_index("tensor"), lax.axis_index("dp")
    z, c = lax.div(t, 2), lax.rem(t, 2)
    x, y = lax.div(d, NY), lax.rem(d, NY)

    def zdev(k):
        return {"tensor": lax.rem(z + k + NZ, NZ) * 2 + c}

    def xdev(k):
        return {"dp": lax.rem(x + k + NX, NX) * NY + y}

    def ydev(k):
        return {"dp": x * NY + lax.rem(y + k + NY, NY)}

    sibling = {"tensor": z * 2 + (1 - c)}

    def copy(src, dst, ss, rs, dev):
        return pltpu.make_async_remote_copy(
            src_ref=src, dst_ref=dst, send_sem=ss, recv_sem=rs, device_id=dev, device_id_type=MESH
        )

    fetch = [
        pltpu.make_async_copy(src, dst, in_sem.at[n])
        for n, (src, dst) in enumerate([
            (og_hbm, og), (w_hbm.at[:, pl.ds(pl.multiple_of(x * 32 + lax.div(y, 4) * 16, 16), 16), :], slab), (hb_hbm, hb),
            (live_hbm, live), (rc_hbm, rc), (gate_hbm, gate), (up_hbm, up),
        ])
    ]
    for cp in fetch:
        cp.start()

    barrier = pltpu.get_barrier_semaphore()

    def greet(s, carry):
        pl.semaphore_signal(barrier, inc=1, device_id={"tensor": lax.rem(t + s, NT)}, device_id_type=MESH)
        return carry

    lax.fori_loop(1, NT, greet, 0)
    for k in (1, 2, 3):
        pl.semaphore_signal(barrier, inc=1, device_id=xdev(k), device_id_type=MESH)
    for k in range(1, NY):
        pl.semaphore_signal(barrier, inc=1, device_id=ydev(k), device_id_type=MESH)
    pend = []

    fetch[0].wait()
    og_all[2 * t] = og[:, :B]
    og_all[2 * t + 1] = og[:, B:]
    pl.semaphore_wait(barrier, NT - 1 + NX - 1 + NY - 1)

    def zslot(k, cc, h):
        return 2 * (lax.rem(z + k + NZ, NZ) * 2 + cc) + h

    class Ring:
        def __init__(self, radius, slot, dev, send, recv, ks=(2, 1)):
            self.ks = ks
            self.radius, self.slot, self.dev, self.send, self.recv = radius, slot, dev, send, recv

        def chunks(self, s):
            return [(0, 0), (1, 1), (0, 1), (1, 0)][: 4 if s < self.radius else 2 if s == self.radius else 0]

        def copy(self, s, k, e, h):
            sg = 1 if e == 0 else -1
            slot = self.slot(-sg * s, h)
            return copy(slot, slot, self.send.at[e, s + k - 1, h], self.recv.at[e, s + k - 1, h], self.dev(sg * k))

        def start(self, s, e, h, ks):
            for k in ks:
                if (e, h) in self.chunks(s + k):
                    cp = self.copy(s, k, e, h)
                    cp.start()
                    pend.append(cp)

        def open(self):
            for k in self.ks:
                for e, h in self.chunks(1):
                    self.start(0, e, h, (k,))

        def step(self, s, arrived=None):
            for e, h in self.chunks(s):
                sg = 1 if e == 0 else -1
                slot = self.slot(-sg * s, h)
                copy(slot, slot, self.send.at[e, s - 1, h], self.recv.at[e, s - 1, h], self.dev(sg)).wait_recv()
                if s % len(self.ks) == 0:
                    self.start(s, e, h, self.ks)
                if arrived is not None:
                    arrived(s, e, h)

    z_ring = Ring(RZ, lambda k, h: og_all.at[zslot(k, c, h)], zdev, z_send, z_recv)

    def sib_start(s, e, h):
        sg = 1 if e == 0 else -1
        slot = og_all.at[zslot(-sg * s, c, h)]
        cp = copy(slot, slot, s_send.at[e, s, h], s_recv.at[e, s, h], sibling)
        cp.start()
        pend.append(cp)

    def sib_wait(s, e, h):
        sg = 1 if e == 0 else -1
        slot = og_all.at[zslot(-sg * s, 1 - c, h)]
        copy(slot, slot, s_send.at[e, s, h], s_recv.at[e, s, h], sibling).wait_recv()

    def z_step(s):
        z_ring.step(s, sib_start)

    z_ring.open()
    for h in (0, 1):
        sib_start(0, 0, h)

    for cp in fetch[1:5]:
        cp.wait()
    r_out = lax.broadcasted_iota(jnp.int32, (64, 192), 0)
    r_in = lax.broadcasted_iota(jnp.int32, (64, 192), 1)
    q = lax.rem(r_out, 16)
    pick = (
        (lax.div(r_out, 16) == lax.div(r_in, 48))
        & (lax.div(q, 4) == lax.div(lax.rem(r_in, 48), 16))
        & (q < 12)
        & (lax.rem(y, 4) * 4 + lax.rem(q, 4) == lax.rem(r_in, 16))
    )
    pick = jnp.where(pick, 1.0, 0.0).astype(BF)
    row16 = lax.broadcasted_iota(jnp.int32, (16, B), 0)

    def make_msg(m, carry):
        rows = slab[pl.ds(m * 12, 12)].reshape(192, B)
        picked = jnp.dot(pick, rows, preferred_element_type=F32)
        for u in range(4):
            o = m * 4 + u
            tile = picked[16 * u : 16 * u + 16]
            for s in range(3):
                key = (hb[0, o * 3 + s] - o * ROWS) * 48 + hb[1, o * 3 + s]
                key = jnp.where(s < live[o], key, -1).astype(F32)
                tile = jnp.where(row16 == 12 + s, key, tile)
            msg[o] = tile.astype(BF)
        return carry

    lax.fori_loop(0, NT // 4, make_msg, 0)
    recv[t] = msg[t]

    def a_copy(s):
        o = lax.rem(t + s, NT)
        return copy(msg.at[o], recv.at[t], a_send.at[s], a_recv.at[t], {"tensor": o})

    def a_start(s, carry):
        a_copy(lax.rem(s + NZ - 1, NT)).start()
        return carry

    lax.fori_loop(1, NT // 2 + 1, a_start, 0)
    lax.fori_loop(NT // 2 + 2, NT + 1, a_start, 0)

    z_step(2)

    for cp in fetch[5:]:
        cp.wait()
    o_row = lax.broadcasted_iota(jnp.int32, (B, B), 0)
    o_col = lax.broadcasted_iota(jnp.int32, (B, B), 1)
    to_y = (
        (lax.div(o_row, 16) == lax.rem(lax.div(o_col, 4), NY))
        & (lax.rem(lax.div(o_row, 4), NX) == lax.div(o_col, 32))
        & (lax.rem(o_row, 4) == lax.rem(o_col, 4))
    )
    to_y = jnp.where(to_y, 1.0, 0.0).astype(BF)
    for i in range(ROWS):
        g = gate[:, i * B : (i + 1) * B].astype(F32)
        u = up[:, i * B : (i + 1) * B].astype(F32)
        sig = 1.0 / (1.0 + jnp.exp(-g))
        a = g * sig
        hid = (a * u).T.astype(BF)
        hid_t[0, i] = hid
        hid_t[1, i] = jnp.dot(to_y, hid, preferred_element_type=F32).astype(BF)

    lane = lax.broadcasted_iota(jnp.int32, (8, 2 * B), 1)
    block_of = lax.div(lane, 4)
    keycol = jnp.full((8, 2 * B), -100.0, F32)
    for n in range(ROWS * KEEP):
        i, k = (n // 8, n % 8) if n < 40 else ((n - 40) // 4, 8 + n % 4)
        v = (i * 48 + rc[i, k]) * 4
        keycol = jnp.where(block_of == n, v.astype(F32), keycol)
    keycol = (keycol + lax.rem(lane, 4).astype(F32))[0:1]


    def a_wait(s, carry):
        h = lax.rem(t + s, NT)
        copy(msg.at[h], recv.at[h], a_send.at[s], a_recv.at[h], {"tensor": h}).wait_recv()
        return carry

    lax.fori_loop(1, NT, a_wait, 0)

    got = recv[...]
    gotf = got.astype(F32)
    rr = lax.broadcasted_iota(jnp.int32, (NT, 16, B), 1)
    keyrow = jnp.where(
        rr < 4, gotf[:, 12:13, :], jnp.where(rr < 8, gotf[:, 13:14, :], jnp.where(rr < 12, gotf[:, 14:15, :], -1000.0))
    )
    keyrow = (keyrow * 4.0 + lax.rem(rr, 4).astype(F32)).reshape(NT * 16, B)
    got = got.reshape(NT * 16, B)
    for v in range(2):
        hot = jnp.where(keyrow == keycol[:, v * B : (v + 1) * B], 1.0, 0.0).astype(BF)
        res = lax.dot_general(hot, got, (((0,), (0,)), ((), ())), preferred_element_type=F32).astype(BF)
        if v == 0:
            comm_y[y, 0:8] = res.reshape(8, 16, B)
        else:
            comm_y[y, 8:10] = res[:32].reshape(2, 16, B)
            comm_x[x] = res[32:112].reshape(5, 16, B)

    y_ring = Ring(
        RY,
        lambda k, h: comm_y.at[lax.rem(y + k + NY, NY), pl.ds(5 * h, 5)],
        ydev, gy_send, gy_recv,
    )
    wy_ring = Ring(RY, lambda k, h: w_b.at[lax.rem(y + k + NY, NY), h], ydev, wy_send, wy_recv, (1,))

    def c_copy(k, back):
        slot = comm_x.at[lax.rem(x - back + NX, NX)]
        return copy(slot, slot, c_send.at[k - 1], c_recv.at[k - 1], xdev(k))

    for k in (2, 1, 3):
        cp = c_copy(k, 0)
        cp.start()
        pend.append(cp)
    y_ring.open()

    z_step(4)
    for k in (1, 3, 2):
        c_copy(k, k).wait_recv()
    s_row = lax.broadcasted_iota(jnp.int32, (64, 64), 0)
    s_col = lax.broadcasted_iota(jnp.int32, (64, 64), 1)
    swap_x = (
        (lax.div(s_row, 16) == lax.rem(lax.div(s_col, 4), 4))
        & (lax.rem(lax.div(s_row, 4), NX) == lax.div(s_col, 16))
        & (lax.rem(s_row, 4) == lax.rem(s_col, 4))
    )
    swap_x = jnp.where(swap_x, 1.0, 0.0).astype(BF)
    for i in range(ROWS):
        res = jnp.dot(swap_x, comm_x[:, i].reshape(64, B), preferred_element_type=F32).astype(BF)
        for u in range(4):
            w_b[y, u // 2, i, :, (u % 2) * B : (u % 2 + 1) * B] = res[16 * u : 16 * u + 16]
    wy_ring.open()
    y_ring.step(2)
    z_step(1)
    z_step(3)
    z_step(6)
    z_step(5)
    for h in (0, 1):
        sib_wait(0, 0, h)
    for s in range(1, RZ + 1):
        for e, h in z_ring.chunks(s):
            sib_wait(s, e, h)

    def products(half):
        def one(i, carry):
            for p in range(2):
                k = half * HALF + 3 * p
                three = jnp.concatenate([og_all[rc[i, k + m]] for m in range(3)], axis=1)
                res = jnp.dot(hid_t[half, i], three, preferred_element_type=F32).astype(BF)
                if half == 0:
                    part_a[:, p, i] = res.reshape(NX, 32, TRI)
                else:
                    part_b[:, p, i] = res.reshape(NY, 16, TRI)
            return carry

        lax.fori_loop(0, ROWS, one, 0)

    def xi(k):
        return lax.rem(x + k + NX, NX)

    def yi(k):
        return lax.rem(y + k + NY, NY)

    def rx(e, j, src, dst):
        return copy(src, dst, rx_send.at[e, j], rx_recv.at[e, j], xdev(1 if e == 0 else -1))

    def begin(cp):
        cp.start()
        pend.append(cp)

    def far(e):
        sg = 1 if e == 0 else -1
        return copy(part_b.at[yi(4), e], far_y.at[e], far_send.at[e], far_recv.at[e], ydev(2 * sg))

    def near(e, p):
        sg = 1 if e == 0 else -1
        return copy(part_b.at[yi(3 * sg), p], near_y.at[e, p], near_send.at[e, p], near_recv.at[e, p], ydev(sg))

    def one_hop(e, p):
        sg = 1 if e == 0 else -1
        return copy(part_b.at[yi(sg), p], one_y.at[e, p], one_send.at[e, p], one_recv.at[e, p], ydev(sg))

    def two_hops(e, p):
        sg = 1 if e == 0 else -1
        return copy(snd_two.at[e, p], two_y.at[e, p], two_send.at[e, p], two_recv.at[e, p], ydev(2 * sg))

    products(1)
    for e in (0, 1):
        begin(far(e))
    for p in (0, 1):
        for e in (0, 1):
            begin(near(e, e if p == 0 else 1 - e))
    products(0)
    begin(rx(0, 0, part_a.at[xi(2), 0], buf_x.at[0]))
    begin(rx(1, 0, part_a.at[xi(2), 1], buf_x.at[1]))
    begin(rx(0, 1, part_a.at[xi(1), 1], fin_x.at[0, 1]))
    begin(rx(1, 1, part_a.at[xi(-1), 0], fin_x.at[1, 0]))
    for p in (0, 1):
        for e in (0, 1):
            begin(one_hop(e, p))

    wy_ring.step(1)
    y_ring.step(1)
    y_ring.step(3)
    y_ring.step(4)
    swap = (
        (lax.div(o_row, 32) == lax.rem(lax.div(o_col, 4), 4))
        & (lax.rem(lax.div(o_row, 4), NY) == lax.div(o_col, 16))
        & (lax.rem(o_row, 4) == lax.rem(o_col, 4))
    )
    swap = jnp.where(swap, 1.0, 0.0).astype(BF)
    for g in range(10):
        res = jnp.dot(swap, comm_y[:, g].reshape(B, B), preferred_element_type=F32).astype(BF)
        for u in range(4):
            n = 4 * g + u
            i, k = n // 8, n % 8
            w_all[x, k // 2, i, :, (k % 2) * B : (k % 2 + 1) * B] = res[32 * u : 32 * u + 32]

    def gx(s, e, q, back):
        sg = 1 if e == 0 else -1
        slot = w_all.at[xi(-sg * back), q]
        return copy(slot, slot, gx_send.at[e, s - 1, q], gx_recv.at[e, s - 1, q], xdev(sg))

    x_all = [(0, 0), (1, 2), (0, 1), (1, 3), (0, 2), (1, 0), (0, 3), (1, 1)]
    for e, q in x_all:
        begin(gx(1, e, q, 0))
    wy_ring.step(2)

    for p in (0, 1):
        for e in (0, 1):
            q = 1 - e if p == 0 else e
            near(e, q).wait_recv()
            sg = 1 if e == 0 else -1
            v = part_b[yi(2 * sg), q].astype(F32) + near_y[e, q].astype(F32)
            if q == e:
                far(e).wait_recv()
                v = v + far_y[e].astype(F32)
            snd_two[e, q] = v.astype(BF)
            begin(two_hops(e, q))
    for e in (0, 1):
        rx(e, 0, part_a.at[xi(2), e], buf_x.at[e]).wait_recv()
        v = part_a[xi(1 if e == 0 else -1), e].astype(F32) + buf_x[e].astype(F32)
        snd_x[e] = v.astype(BF)
        begin(rx(e, 2, snd_x.at[e], fin_x.at[e, e]))
    wy_ring.step(3)

    def scatter(own, groups, dst, i):
        low = lax.broadcasted_iota(jnp.int32, (groups, 8, B), 1) < 4
        own = own.reshape(groups, 8, HALF * B)
        for p in range(HALF // 2):
            a0 = own[:, :, 2 * p * B : (2 * p + 1) * B]
            a1 = own[:, :, (2 * p + 1) * B : (2 * p + 2) * B]
            first = (i * HALF + 2 * p) * 4
            dst[:, 0, first : first + 8, :] = jnp.where(low, a0, pltpu.roll(a1, 4, 1))
            dst[:, 1, first : first + 8, :] = jnp.where(low, pltpu.roll(a0, 4, 1), a1)

    for e in (0, 1):
        rx(e, 1, part_a.at[xi(1), 1 - e], fin_x.at[e, 1 - e]).wait_recv()
        rx(e, 2, snd_x.at[e], fin_x.at[e, e]).wait_recv()
    yin[:, :, HROW:, :] = jnp.zeros((NY // 2, 2, B - HROW, B), F32)
    for i in range(ROWS):
        own = [
            part_a[x, p, i].astype(F32) + fin_x[0, p, i].astype(F32) + fin_x[1, p, i].astype(F32) for p in (0, 1)
        ]
        scatter(jnp.concatenate(own, axis=1), NY // 2, yin, i)
    snd_ya[...] = yin[...].reshape(NY, B, B).astype(BF)

    def ya(k):
        return copy(snd_ya.at[yi(k)], rcv_ya.at[k - 1], ya_send.at[k - 1], ya_recv.at[k - 1], ydev(k))

    for k in (4, 3, 5, 2, 6, 1, 7):
        begin(ya(k))

    for e, q in x_all:
        gx(1, e, q, 1).wait_recv()
        if (e, q) in x_all[:4]:
            begin(gx(2, e, q, 1))


    for e in (0, 1):
        for p in (0, 1):
            one_hop(e, p).wait_recv()
            two_hops(e, p).wait_recv()
    xin[:, :, HROW:, :] = jnp.zeros((NX // 2, 2, B - HROW, B), F32)
    for i in range(ROWS):
        own = [
            part_b[y, p, i].astype(F32) + one_y[0, p, i].astype(F32) + one_y[1, p, i].astype(F32)
            + two_y[0, p, i].astype(F32) + two_y[1, p, i].astype(F32)
            for p in (0, 1)
        ]
        scatter(jnp.concatenate(own, axis=1), NX // 2, xin, i)
    snd_xb[...] = xin[...].reshape(NX, B, B).astype(BF)

    def xb(k):
        return copy(snd_xb.at[xi(k)], rcv_xb.at[k - 1], xb_send.at[k - 1], xb_recv.at[k - 1], xdev(k))

    for k in (2, 1, 3):
        begin(xb(k))

    for e, q in x_all[:4]:
        gx(2, e, q, 2).wait_recv()

    wy_ring.step(4)

    def hidden_grad(i, carry):
        total = jnp.zeros((B, B), F32)
        for q in range(6):
            left = jnp.concatenate([og_all[rc[i, q * 2 + m]] for m in range(2)], axis=1)
            if q < 4:
                right = w_all[:, q, i].reshape(B, 2 * B)
            else:
                right = w_b[:, q - 4, i].reshape(B, 2 * B)
                right = jnp.dot(swap, right, preferred_element_type=F32).astype(BF)
            total = total + lax.dot_general(left, right, (((1,), (1,)), ((), ())), preferred_element_type=F32)
        cols = pl.ds(pl.multiple_of(i * B, B), B)
        hg[:, cols] = total
        return carry

    lax.fori_loop(0, ROWS, hidden_grad, 0)
    hg_out = pltpu.make_async_copy(hg, hg_hbm, out_sem.at[0])
    hg_out.start()

    for half, n, mine, box, cps in (
        (0, NY, yin[lax.div(y, 2), lax.rem(y, 2)], rcv_ya, ya),
        (1, NX, xin[lax.div(x, 2), lax.rem(x, 2)], rcv_xb, xb),
    ):
        for k in range(1, n):
            cps(k).wait_recv()
            mine = mine + box[k - 1].astype(F32)
        for i in range(ROWS):
            first = (i * KEEP + half * HALF) * 4
            wgf[first : first + 4 * HALF, :] = mine[i * 4 * HALF : (i + 1) * 4 * HALF]
    for a in range(4):
        wg[:, a * B : (a + 1) * B] = wgf[pl.ds(a, ROWS * KEEP, stride=4), :].astype(BF)
    wg_out = pltpu.make_async_copy(wg, wg_hbm, out_sem.at[1])
    wg_out.start()

    def a_done(s, carry):
        a_copy(s).wait_send()
        return carry

    lax.fori_loop(1, NT, a_done, 0)
    for cp in pend:
        cp.wait_send()
    for cp in (hg_out, wg_out):
        cp.wait()


def local(gate_pre, up_pre, out_grad, weight_slots, holder_blocks, holder_live_slots, row_columns):
    hbm = pl.BlockSpec(memory_space=pl.ANY)
    dma = pltpu.SemaphoreType.DMA
    hidden_grad, weight_grad = pl.pallas_call(
        kernel,
        out_shape=(
            jax.ShapeDtypeStruct(gate_pre.shape, F32),
            jax.ShapeDtypeStruct((ROWS * KEEP, 4 * B), BF),
        ),
        in_specs=[hbm] * 7,
        out_specs=(hbm, hbm),
        scratch_shapes=[
            pltpu.VMEM(gate_pre.shape, BF), pltpu.VMEM(up_pre.shape, BF), pltpu.VMEM(out_grad.shape, BF),
            pltpu.SMEM((2, 3 * NT), jnp.int32), pltpu.SMEM((NT,), jnp.int32), pltpu.SMEM((ROWS, KEEP), jnp.int32),
            pltpu.VMEM(gate_pre.shape, F32), pltpu.VMEM((ROWS * KEEP, 4 * B), BF),
            pltpu.VMEM((2 * NT, B, B), BF),
            pltpu.VMEM((3 * NT, 16, B), BF),
            pltpu.VMEM((NT, 16, B), BF),
            pltpu.VMEM((NT, 16, B), BF),
            pltpu.VMEM((NY, 10, 16, B), BF),
            pltpu.VMEM((NX, 5, 16, B), BF),
            pltpu.VMEM((NX, 4, ROWS, 32, 2 * B), BF),
            pltpu.VMEM((NY, 2, ROWS, 16, 2 * B), BF),
            pltpu.VMEM((2, ROWS, B, B), BF),
            pltpu.VMEM((NX, 2, ROWS, 32, TRI), BF),
            pltpu.VMEM((NY, 2, ROWS, 16, TRI), BF),
            pltpu.VMEM((2, ROWS, 32, TRI), BF),
            pltpu.VMEM((2, 2, ROWS, 32, TRI), BF),
            pltpu.VMEM((2, ROWS, 32, TRI), BF),
            pltpu.VMEM((2, ROWS, 16, TRI), BF),
            pltpu.VMEM((2, 2, ROWS, 16, TRI), BF),
            pltpu.VMEM((2, 2, ROWS, 16, TRI), BF),
            pltpu.VMEM((2, 2, ROWS, 16, TRI), BF),
            pltpu.VMEM((2, 2, ROWS, 16, TRI), BF),
            pltpu.VMEM((NY // 2, 2, B, B), F32),
            pltpu.VMEM((NY, B, B), BF), pltpu.VMEM((NY - 1, B, B), BF),
            pltpu.VMEM((NX // 2, 2, B, B), F32),
            pltpu.VMEM((NX, B, B), BF), pltpu.VMEM((NX - 1, B, B), BF),
            pltpu.VMEM((NROW, B), F32),
            dma((7,)), dma((2,)),
            dma((2, RZ, 2)), dma((2, RZ, 2)),
            dma((2, RZ + 1, 2)), dma((2, RZ + 1, 2)),
            dma((NT,)), dma((NT,)),
            dma((2, RY, 2)), dma((2, RY, 2)),
            dma((2, 2, 4)), dma((2, 2, 4)),
            dma((NX - 1,)), dma((NX - 1,)), dma((2, RY, 2)), dma((2, RY, 2)),
            dma((2, 3)), dma((2, 3)),
            dma((2,)), dma((2,)), dma((2, 2)), dma((2, 2)),
            dma((2, 2)), dma((2, 2)), dma((2, 2)), dma((2, 2)),
            dma((NY - 1,)), dma((NY - 1,)), dma((NX - 1,)), dma((NX - 1,)),
        ],
        compiler_params=pltpu.CompilerParams(
            collective_id=0, has_side_effects=True, vmem_limit_bytes=62 * 1024 * 1024
        ),
        cost_estimate=pl.CostEstimate(flops=600_000_000, bytes_accessed=4_000_000, transcendentals=82_000),
    )(gate_pre, up_pre, out_grad, weight_slots, holder_blocks.T, holder_live_slots, row_columns)
    g, u = gate_pre.astype(F32), up_pre.astype(F32)
    sig = jax.nn.sigmoid(g)
    gate_grad = (hidden_grad * u * (sig * (1.0 + g * (1.0 - sig)))).astype(BF)
    up_grad = (hidden_grad * (g * sig)).astype(BF)
    return gate_grad, up_grad, weight_grad


def solution(mesh):
    placed = (
        P("dp", "tensor"),
        P("dp", "tensor"),
        P("dp", "tensor"),
        P("tensor", None, None),
        P("tensor", None),
        P("tensor"),
        P("tensor", None),
    )
    return jax.shard_map(
        local,
        mesh=mesh,
        in_specs=placed,
        out_specs=(P("dp", "tensor"), P("dp", "tensor"), P("tensor", "dp")),
        check_vma=False,
    )
```
